512 devices in a mesh: ctx: 8 (over x, y_hi), head: 32 (over z, y_lo), pool: 2 (over core).
Axes of the slice: x: 4, y: 8 (y_hi: 2, y_lo: 4; y = y_hi * 4 + y_lo), z: 8, core: 2. Of those that a mesh axis runs over, the one named last changes fastest.
Arguments:
- queries: bfloat16 [2, 1024, 64, 576], P('pool', 'ctx', 'head')
- new_latent: bfloat16 [2, 1024, 576], P('pool', 'ctx')
- cache_pool: bfloat16 [8, 32, 64, 576], P('ctx', 'pool'), may hold values from -6 to 6
- block_list: int32 [2, 8, 16], P('pool', 'ctx'), may hold values from 0 to 31, as said below
- cached_lengths: int32 [2], P('pool'), may hold values from 2730 to 8192
- w_uv: bfloat16 [64, 512, 128], P('head'), may hold values from -4 to 4
- w_o: bfloat16 [64, 128, 7168], P('head'), may hold values from -0.125 to 0.125
Outputs:
- mixed: bfloat16 [2, 1024, 7168], P('pool', 'ctx', 'head')
The draws below stay inside these ranges and needn't reach their ends.
Inputs may be any that keep to these rules, and one draw needn't show every extreme that they name: For each ctx index c, block_list[:, c, :] holds every slot 0 to 31 exactly once.
All inputs are finite; a program needn't handle non-finite values.
Results may differ from the reference program's by a relative error of at most 0.015.
Values may be sent and summed in bfloat16 or wider, within the bound.
A program may use at most 64 MiB of HBM per device.

```python
import jax
import jax.numpy as jnp
from jax import lax

D = 7168
HEADS = 64
LAT = 512
ROPE = 64
VH = 128
BLK = 64
NEWDEV = 128
HB = 16
CONVS = 2
NEW = 1024
HIST = 8192
SLOTS = 32
N_CTX = 8


def shared_latent(key):
    base = jax.random.normal(jax.random.fold_in(key, 1), (CONVS, NEW, LAT + ROPE), jnp.float32)
    return base


def draw_new_latent(key, part):
    base = shared_latent(key)
    latent = base
    return latent.astype(jnp.bfloat16)


def draw_queries(key, part):
    key = jax.random.fold_in(key, 22)
    shape_q = (CONVS, NEW, HEADS, LAT + ROPE)
    query_vals = jax.random.normal(key, shape_q, jnp.float32)
    return query_vals.astype(jnp.bfloat16)


def draw_block_list(key, part):
    key = jax.random.fold_in(key, 11)
    cycle_size = NEW // NEWDEV
    cycle_keys = jax.random.split(key, cycle_size)
    orders = jax.vmap(lambda one_key: jax.random.permutation(one_key, SLOTS))(cycle_keys)
    orders = orders.astype(jnp.int32).reshape(cycle_size, CONVS, HB)
    return jnp.transpose(orders, (1, 0, 2))


def draw_cached_lengths(key, part):
    key = jax.random.fold_in(key, 12)
    longest = jax.random.randint(jax.random.fold_in(key, 1), (), 0, CONVS)
    others = jax.random.randint(jax.random.fold_in(key, 2), (CONVS,), HIST // 3, HIST + 1)
    conv_ids = jnp.arange(CONVS, dtype=jnp.int32)
    return jnp.where(conv_ids == longest, HIST, others).astype(jnp.int32)


def with_spikes(values, own_key, source, target, parts, factor):
    owner, partner = [(jnp.arange(values.shape[axis_at]) // (values.shape[axis_at] // parts)).reshape([-1 if axis == axis_at else 1 for axis in range(values.ndim)]) for axis_at in (source, target)]
    chosen = jax.random.permutation(own_key, parts)[partner]
    strong = (owner == chosen) | (owner == (partner + parts // 2) % parts)
    return jnp.where(strong, factor * values, values)


def shard_levels(stream_key, shape, pieces, least, high):
    def one(dim, shards_of):
        heights = jax.random.uniform(jax.random.fold_in(jax.random.fold_in(stream_key, 6), dim), (shards_of,), jnp.float32, least / len(pieces), high / len(pieces))
        return jnp.repeat(jnp.exp(heights), shape[dim] // shards_of).reshape((-1,) + (1,) * (len(shape) - dim - 1))

    factor_of = one(*pieces[0])
    for cut in pieces[1:]:
        factor_of = factor_of * one(*cut)
    return factor_of


def centred(rng, dims, scale, bound, cuts=(), kind=jnp.bfloat16):
    entries = scale * jax.random.normal(rng, dims, jnp.float32)
    if cuts:
        entries = entries * shard_levels(rng, dims, cuts, -0.22, 0.18)
    return jnp.clip(entries, -bound, bound).astype(kind)


def heavy_noise(key, extent, width, limit, cuts, heavy, kind=jnp.bfloat16):
    values = width * jax.random.normal(key, extent, jnp.float32)
    if cuts:
        values = values * shard_levels(key, extent, cuts, -0.22, 0.18)
    return jnp.clip(with_spikes(values, jax.random.fold_in(key, 3), *heavy), -limit, limit).astype(kind)


def setup_inputs(seed: int = 0) -> dict:
    splits = jax.random.split(jax.random.key(seed), 8)
    return {
        "queries": draw_queries(jax.random.fold_in(splits[7], 71), 0),
        "new_latent": draw_new_latent(jax.random.fold_in(splits[7], 71), 0),
        "cache_pool": centred(splits[2], (N_CTX, SLOTS, BLK, LAT + ROPE), 1.0, 6.0, ((0, 8), (1, 2))),
        "block_list": draw_block_list(jax.random.fold_in(splits[7], 71), 0),
        "cached_lengths": draw_cached_lengths(jax.random.fold_in(splits[7], 71), 0),
        "w_uv": centred(splits[5], (HEADS, LAT, VH), 0.25, 4.0, ((0, 32),)),
        "w_o": heavy_noise(splits[6], (HEADS, VH, D), (HEADS * VH) ** -0.5, 0.125, ((0, 32),), (0, 2, 32, 2.75)),
    }


score_scale = 192.0 ** -0.5
neg_big = -1e30


def one_conversation(query_conv, latent_conv, cache_pool, blocks_conv, cached):
    cycle_ids = jnp.arange(cache_pool.shape[0], dtype=jnp.int32)
    history = cache_pool[cycle_ids[:, None], blocks_conv]
    history = history.reshape(HIST, LAT + ROPE)
    key_latent = jnp.concatenate([history, latent_conv], axis=0)
    key_rows = jnp.arange(HIST + NEW, dtype=jnp.int32)
    query_rows = jnp.arange(NEW, dtype=jnp.int32)
    visible = jnp.where((key_rows < HIST)[None, :], (key_rows < cached)[None, :],
                        (key_rows - HIST)[None, :] <= query_rows[:, None])
    value_part = key_latent[:, :LAT].astype(jnp.float32)

    def per_head(query_head):
        scores = jnp.dot(query_head, key_latent.T, preferred_element_type=jnp.float32) * score_scale
        scores = jnp.where(visible, scores, neg_big)
        row_max = jnp.max(scores, axis=1, keepdims=True)
        weights = jnp.where(visible, jnp.exp(scores - row_max), 0.0)
        denominator = jnp.sum(weights, axis=1, keepdims=True)
        latent_out = jnp.dot(weights, value_part, preferred_element_type=jnp.float32) / denominator
        return latent_out.astype(jnp.bfloat16)

    latent_out = lax.map(per_head, jnp.transpose(query_conv, (1, 0, 2)))
    return latent_out


def reference(queries, new_latent, cache_pool, block_list, cached_lengths, w_uv, w_o):
    results = []
    for conv_index in range(CONVS):
        latent_out = one_conversation(queries[conv_index], new_latent[conv_index], cache_pool,
                                      block_list[conv_index], cached_lengths[conv_index])
        head_out = jnp.einsum('hnl,hlv->nhv', latent_out.astype(jnp.float32), w_uv.astype(jnp.float32))
        head_out = head_out.astype(jnp.bfloat16)
        mixed_conv = jnp.dot(head_out.reshape(NEW, HEADS * VH), w_o.reshape(HEADS * VH, D),
                             preferred_element_type=jnp.float32)
        results.append(mixed_conv.astype(jnp.bfloat16))
    return jnp.stack(results, axis=0)
```

```python
import jax
import jax.numpy as jnp
from jax import lax
from jax.experimental import pallas as pl
from jax.experimental.pallas import tpu as pltpu
from jax.sharding import PartitionSpec as P

MESH = pl.DeviceIdType.MESH
LAT = 512
VH = 128
UNIT = 32
SCALE = 192.0 ** -0.5 * 1.4426950408889634
NEG = -1e30
F32 = jnp.float32
BF16 = jnp.bfloat16


def place():
    c, h, p = lax.axis_index("ctx"), lax.axis_index("head"), lax.axis_index("pool")
    return c // 2, c % 2, h // 4, h % 4, p


def device(x, yh, z, yl, p):
    return {"ctx": x * 2 + yh, "head": z * 4 + yl, "pool": p}


def greet(others):
    barrier = pltpu.get_barrier_semaphore()
    for other in others:
        pl.semaphore_signal(barrier, inc=1, device_id=other, device_id_type=MESH)
    pl.semaphore_wait(barrier, len(others))


def remote(src, dst, send, recv, to):
    return pltpu.make_async_remote_copy(
        src_ref=src, dst_ref=dst, send_sem=send, recv_sem=recv, device_id=to, device_id_type=MESH
    )


def attention_kernel(
    blocks, cached_ref, q_in, new_in, pool_in, w_uv,
    out,
    qbuf, pbuf, kbuf, vt, wt, acc, stat, ores, orecv, srecv,
    lsem, psem, qs, qr, ups, upr, dns, dnr, zus, zur, zds, zdr, os_, or_, ss, sr,
):
    x, yh, z, yl, p = place()
    b = z % 2
    xu, xd, xo = (x + 1) % 4, (x + 3) % 4, (x + 2) % 4
    at_core = device(x, yh, z, yl, 1 - p)
    at_xu, at_xd, at_xo = [device(k, yh, z, yl, p) for k in (xu, xd, xo)]
    y_up, y_dn = (yh * 4 + yl + 1) % 8, (yh * 4 + yl + 7) % 8
    at_yu, at_yd = [device(x, k // 4, z, k % 4, p) for k in (y_up, y_dn)]
    at_zu, at_zd = [device(x, yh, k % 8, yl, p) for k in (z + 1, z + 7)]
    cached = cached_ref[0]
    half = 16

    mine = pl.ds(p * half, half)
    local = [
        pltpu.make_async_copy(pool_in, pbuf.at[mine], lsem.at[0]),
        pltpu.make_async_copy(q_in, qbuf.at[0], lsem.at[1]),
        pltpu.make_async_copy(new_in, kbuf.at[0, pl.ds(32, 4)], lsem.at[2]),
    ]
    for copy in local:
        copy.start()
    greet([at_core, at_xu, at_xd, at_xo, at_yu, at_yd, at_zu, at_zd])

    push = remote(pool_in, pbuf.at[mine], psem.at[0], psem.at[1], at_core)
    push.start()
    q_up = remote(q_in, qbuf.at[1], qs.at[0], qr.at[0], at_xu)
    q_dn = remote(q_in, qbuf.at[2], qs.at[1], qr.at[1], at_xd)
    q_up.start()
    q_dn.start()
    q_up2 = remote(qbuf.at[1, pl.ds(0, 128)], qbuf.at[3, pl.ds(0, 128)], qs.at[2], qr.at[2], at_xu)
    q_dn2 = remote(qbuf.at[2, pl.ds(128, 128)], qbuf.at[3, pl.ds(128, 128)], qs.at[3], qr.at[3], at_xd)

    for h in range(2):
        wt[h] = w_uv[h].T

    for copy in local:
        copy.wait()
    push.wait_recv()

    def gather(k, carry):
        kbuf[0, pl.ds(2 * k, 2)] = pbuf[blocks[k]].reshape(2, UNIT, kbuf.shape[-1])
        return carry

    lax.fori_loop(0, half, gather, 0)

    def y_up_copy(s, j):
        u = b * 18 + j
        return remote(kbuf.at[s, u], kbuf.at[1, u], ups.at[j], upr.at[j], at_yu)

    def y_dn_copy(s, j):
        u = b * 18 + 9 + j
        return remote(kbuf.at[s, u], kbuf.at[1, u], dns.at[j], dnr.at[j], at_yd)

    def z_up_copy(j, base):
        u = base * 18 + j
        return remote(kbuf.at[1, u], kbuf.at[1, u], zus.at[j], zur.at[j], at_zu)

    def z_dn_copy(j, base):
        u = base * 18 + 9 + j
        return remote(kbuf.at[1, u], kbuf.at[1, u], zds.at[j], zdr.at[j], at_zd)

    @pl.when(yl == 3)
    def _():
        for j in range(9):
            y_up_copy(0, j).start()

    @pl.when(yl == 0)
    def _():
        for j in range(9):
            y_dn_copy(0, j).start()

    def forward(j):
        y_up_copy(1, j).wait_recv()

        @pl.when(yl != 3)
        def _():
            y_up_copy(1, j).start()

        z_up_copy(j, b).start()
        y_dn_copy(1, j).wait_recv()

        @pl.when(yl != 0)
        def _():
            y_dn_copy(1, j).start()

        z_dn_copy(j, b).start()

    owners = [x, xd, xu, xo]

    def scores(keys, query, owner, c, first_row):
        s = lax.dot_general(keys, query, (((1,), (1,)), ((), ())), preferred_element_type=F32) * SCALE
        rows = keys.shape[0]
        parts = []
        hist = min(rows, 1024 - first_row)
        if hist:
            row = lax.broadcasted_iota(jnp.int32, (hist, 256), 0)
            parts.append(jnp.where(row < cached - c * 1024 - first_row, s[:hist], NEG))
        if rows - hist:
            row = lax.broadcasted_iota(jnp.int32, (rows - hist, 256), 0)
            token = lax.broadcasted_iota(jnp.int32, (rows - hist, 256), 1) % 128
            parts.append(jnp.where(row - token <= (owner * 2 + yh - c) * 128, s[hist:], NEG))
        return jnp.concatenate(parts, axis=0) if len(parts) > 1 else parts[0]

    def attend(g, owner, s_at, c, unit, units, fresh):
        rows = units * UNIT
        keys = kbuf[s_at, unit:unit + units].reshape(rows, kbuf.shape[-1])
        s = scores(keys, qbuf[g], owner, c, unit * UNIT)
        top = jnp.max(s, axis=0, keepdims=True)
        if not fresh:
            old = stat[g, 0:1]
            top = jnp.maximum(top, old)
        w = jnp.exp2(s - top)
        total = jnp.sum(w, axis=0, keepdims=True)
        o = jnp.dot(vt[s_at, :, unit * UNIT:unit * UNIT + rows], w.astype(BF16), preferred_element_type=F32)
        if not fresh:
            f = jnp.exp2(old - top)
            total = total + f * stat[g, 1:2]
            o = o + f * acc[g]
        stat[g, 0:1] = top
        stat[g, 1:2] = total
        acc[g] = o

    def turn(s_at, unit, units):
        rows = units * UNIT
        v = kbuf[s_at, unit:unit + units].reshape(rows, kbuf.shape[-1])[:, :LAT]
        vt[s_at, :, unit * UNIT:unit * UNIT + rows] = v.T

    c_own, c_far = x * 2 + yh, x * 2 + 1 - yh
    stat[...] = jnp.zeros_like(stat)
    turn(0, 0, 36)
    forward(0)
    forward(1)
    attend(0, owners[0], 0, c_own, 0, 36, True)
    forward(2)
    forward(3)
    q_up.wait_recv()
    q_up2.start()
    q_dn.wait_recv()
    q_dn2.start()
    forward(4)
    attend(1, owners[1], 0, c_own, 0, 36, True)
    forward(5)
    attend(2, owners[2], 0, c_own, 0, 36, True)
    forward(6)
    q_up2.wait_recv()
    q_dn2.wait_recv()
    attend(3, owners[3], 0, c_own, 0, 36, True)
    forward(7)
    forward(8)
    for j in range(9):
        z_up_copy(j, 1 - b).wait_recv()
        z_dn_copy(j, 1 - b).wait_recv()
    turn(1, 0, 36)

    results = []
    for slot, g in enumerate((3, 1, 2, 0)):
        attend(g, owners[g], 1, c_far, 0, 36, False)
        lat = (acc[g] / stat[g, 1:2]).astype(BF16)
        for h in range(2):
            o = jnp.dot(wt[h], lat[:, h * 128:(h + 1) * 128], preferred_element_type=F32)
            ores[g, :, h * 128:(h + 1) * 128] = o.astype(BF16)
        if g:
            to = {1: at_xd, 2: at_xu, 3: at_xo}[g]
            sent = [
                remote(ores.at[g], orecv.at[g - 1], os_.at[g - 1], or_.at[g - 1], to),
                remote(stat.at[g], srecv.at[g - 1], ss.at[g - 1], sr.at[g - 1], to),
            ]
            for copy in sent:
                copy.start()
            results += sent

    for copy in results:
        copy.wait_recv()
    tops = [stat[0, 0:1]] + [srecv[i, 0:1] for i in range(3)]
    sums = [stat[0, 1:2]] + [srecv[i, 1:2] for i in range(3)]
    outs = [ores[0]] + [orecv[i] for i in range(3)]
    top = jnp.maximum(jnp.maximum(tops[0], tops[1]), jnp.maximum(tops[2], tops[3]))
    shares = [t * jnp.exp2(m - top) for m, t in zip(tops, sums)]
    inv = 1.0 / (shares[0] + shares[1] + shares[2] + shares[3])
    head = sum(o.astype(F32) * (s * inv) for o, s in zip(outs, shares))
    for h in range(2):
        out[:, h * 128:(h + 1) * 128] = head[:, h * 128:(h + 1) * 128].T.astype(BF16)

    push.wait_send()
    for copy in (q_up, q_dn, q_up2, q_dn2):
        copy.wait_send()
    for j in range(9):
        y_up_copy(1, j).wait_send()
        y_dn_copy(1, j).wait_send()
        z_up_copy(j, b).wait_send()
        z_dn_copy(j, b).wait_send()
    for copy in results:
        copy.wait_send()


def attention(blocks, cached, q, new, pool, w_uv):
    width = q.shape[-1]
    any_ = pl.BlockSpec(memory_space=pl.ANY)
    smem = pl.BlockSpec(memory_space=pltpu.SMEM)
    vmem = pl.BlockSpec(memory_space=pltpu.VMEM)
    dma = pltpu.SemaphoreType.DMA
    return pl.pallas_call(
        attention_kernel,
        out_shape=jax.ShapeDtypeStruct((128, 256), BF16),
        in_specs=[smem, smem, any_, any_, any_, vmem],
        out_specs=vmem,
        scratch_shapes=[
            pltpu.VMEM((4, 256, width), BF16),
            pltpu.VMEM((32, 64, width), BF16),
            pltpu.VMEM((2, 36, UNIT, width), BF16),
            pltpu.VMEM((2, LAT, 36 * UNIT), BF16),
            pltpu.VMEM((2, VH, LAT), BF16),
            pltpu.VMEM((4, LAT, 256), F32),
            pltpu.VMEM((4, 8, 256), F32),
            pltpu.VMEM((4, VH, 256), BF16),
            pltpu.VMEM((3, VH, 256), BF16),
            pltpu.VMEM((3, 8, 256), F32),
            dma((3,)), dma((2,)), dma((4,)), dma((4,)),
            dma((9,)), dma((9,)), dma((9,)), dma((9,)),
            dma((9,)), dma((9,)), dma((9,)), dma((9,)),
            dma((3,)), dma((3,)), dma((3,)), dma((3,)),
        ],
        compiler_params=pltpu.CompilerParams(
            collective_id=0, has_side_effects=True, vmem_limit_bytes=48 * 2**20
        ),
        cost_estimate=pl.CostEstimate(flops=5 * 10**9, bytes_accessed=4 * 10**6, transcendentals=2 * 10**6),
    )(blocks, cached, q, new, pool, w_uv)


def project_kernel(
    a_ref, w_in, out,
    w, up_out, up_in, dn_out, dn_in, own, y_out, y_in,
    wsem, us, ur, ds, dr, ys, yr,
):
    x, yh, z, yl, p = place()
    at_zu, at_zd = [device(x, yh, k % 8, yl, p) for k in (z + 1, z + 7)]
    at_y = [device(x, yh, z, (yl + d) % 4, p) for d in (1, 2, 3)]
    load = pltpu.make_async_copy(w_in, w, wsem)
    load.start()
    greet([at_zu, at_zd] + at_y)
    load.wait()
    a = a_ref[...]

    def term(dest):
        at = pl.multiple_of((dest % 8) * 896, 128)
        return jnp.dot(a, w[:, pl.ds(at, 896)], preferred_element_type=F32)

    def up(s, r):
        rows = pl.ds(r * 32, 32)
        return remote(up_out.at[s, rows], up_in.at[s, rows], us.at[s, r], ur.at[s, r], at_zu)

    def dn(s, r):
        rows = pl.ds(r * 32, 32)
        return remote(dn_out.at[s, rows], dn_in.at[s, rows], ds.at[s, r], dr.at[s, r], at_zd)

    up_order, dn_order = (2, 3, 0, 1), (0, 1, 2, 3)
    started = []
    for s in range(4):
        if s == 0:
            far = term(z + 4)
            for r in (0, 1):
                up_out[0, r * 32:(r + 1) * 32] = far[r * 32:(r + 1) * 32].astype(BF16)
                started.append(up(0, r))
                started[-1].start()
                r = r + 2
                dn_out[0, r * 32:(r + 1) * 32] = far[r * 32:(r + 1) * 32].astype(BF16)
                started.append(dn(0, r))
                started[-1].start()
            continue
        t_up, t_dn = term(z + 4 - s), term(z + 4 + s)
        for i in range(4):
            for flow, order, t, sent, got, extra in (
                (up, up_order, t_up, up_out, up_in, (0, 1)),
                (dn, dn_order, t_dn, dn_out, dn_in, (2, 3)),
            ):
                r = order[i]
                rows = slice(r * 32, (r + 1) * 32)
                v = t[rows]
                if s > 1 or r in extra:
                    flow(s - 1, r).wait_recv()
                    v = v + got[s - 1, rows].astype(F32)
                sent[s, rows] = v.astype(BF16)
                started.append(flow(s, r))
                started[-1].start()

    t = term(z)
    y_copies = []
    for r in range(4):
        rows = slice(r * 32, (r + 1) * 32)
        up(3, r).wait_recv()
        dn(3, r).wait_recv()
        v = t[rows] + up_in[3, rows].astype(F32) + dn_in[3, rows].astype(F32)
        for k in range(4):
            piece = v[:, k * 224:(k + 1) * 224]
            own[k, rows, 0:224] = piece
            y_out[k, rows, 0:224] = piece.astype(BF16)
        for d in range(3):
            at = pl.ds(r * 32, 32)
            copy = remote(
                y_out.at[(yl + d + 1) % 4, at], y_in.at[d, at], ys.at[d, r], yr.at[d, r], at_y[d]
            )
            copy.start()
            y_copies.append(copy)
    for r in range(4):
        rows = slice(r * 32, (r + 1) * 32)
        for d in range(3):
            y_copies[r * 3 + d].wait_recv()
        v = own[yl, rows, 0:224]
        for d in range(3):
            v = v + y_in[d, rows, 0:224].astype(F32)
        out[rows, :] = v.astype(BF16)
    for copy in started + y_copies:
        copy.wait_send()


def project(a, w_o):
    any_ = pl.BlockSpec(memory_space=pl.ANY)
    vmem = pl.BlockSpec(memory_space=pltpu.VMEM)
    dma = pltpu.SemaphoreType.DMA
    return pl.pallas_call(
        project_kernel,
        out_shape=jax.ShapeDtypeStruct((128, 224), BF16),
        in_specs=[vmem, any_],
        out_specs=vmem,
        scratch_shapes=[
            pltpu.VMEM(w_o.shape, BF16),
            pltpu.VMEM((4, 128, 896), BF16),
            pltpu.VMEM((4, 128, 896), BF16),
            pltpu.VMEM((4, 128, 896), BF16),
            pltpu.VMEM((4, 128, 896), BF16),
            pltpu.VMEM((4, 128, 256), F32),
            pltpu.VMEM((4, 128, 256), BF16),
            pltpu.VMEM((3, 128, 256), BF16),
            dma, dma((4, 4)), dma((4, 4)), dma((4, 4)), dma((4, 4)), dma((3, 4)), dma((3, 4)),
        ],
        compiler_params=pltpu.CompilerParams(
            collective_id=1, has_side_effects=True, vmem_limit_bytes=48 * 2**20
        ),
        cost_estimate=pl.CostEstimate(flops=5 * 10**8, bytes_accessed=4 * 10**6, transcendentals=0),
    )(a, w_o)


def body(queries, new_latent, cache_pool, block_list, cached_lengths, w_uv, w_o):
    width = queries.shape[-1]
    q = jnp.transpose(queries[0], (1, 0, 2)).reshape(256, width)
    new = new_latent[0].reshape(4, UNIT, width)
    a = attention(block_list[0, 0], cached_lengths, q, new, cache_pool[0], w_uv)
    return project(a, w_o.reshape(256, -1))[None]


def solution(mesh):
    in_specs = (
        P("pool", "ctx", "head", None),
        P("pool", "ctx", None),
        P("ctx", "pool", None, None),
        P("pool", "ctx", None),
        P("pool"),
        P("head", None, None),
        P("head", None, None),
    )
    out_specs = P("pool", "ctx", "head")
    return jax.shard_map(body, mesh=mesh, in_specs=in_specs, out_specs=out_specs, check_vma=False)
```

```python
import jax
import jax.numpy as jnp
from jax import lax
from jax.experimental import pallas as pl
from jax.experimental.pallas import tpu as pltpu
from jax.sharding import PartitionSpec as P

MESH = pl.DeviceIdType.MESH
LAT = 512
VH = 128
UNIT = 32
SCALE = 192.0 ** -0.5 * 1.4426950408889634
NEG = -1e30
F32 = jnp.float32
BF16 = jnp.bfloat16


def place():
    c, h, p = lax.axis_index("ctx"), lax.axis_index("head"), lax.axis_index("pool")
    return c // 2, c % 2, h // 4, h % 4, p


def device(x, yh, z, yl, p):
    return {"ctx": x * 2 + yh, "head": z * 4 + yl, "pool": p}


def greet(others):
    barrier = pltpu.get_barrier_semaphore()
    for other in others:
        pl.semaphore_signal(barrier, inc=1, device_id=other, device_id_type=MESH)
    pl.semaphore_wait(barrier, len(others))


def remote(src, dst, send, recv, to):
    return pltpu.make_async_remote_copy(
        src_ref=src, dst_ref=dst, send_sem=send, recv_sem=recv, device_id=to, device_id_type=MESH
    )


def kernel(
    blocks, cached_ref, q_in, new_in, pool_in, w_uv, w_in,
    out,
    qbuf, pbuf, kbuf, newt, vt, wt, acc, stat, ores, orecv, sstat, srecv,
    w, wo, at, up_out, up_in, dn_out, dn_in, own, y_out, y_in,
    lsem, psem, qs, qr, ups, upr, dns, dnr, zus, zur, zds, zdr, os_, or_, ss, sr,
    us, ur, ds, dr, ys, yr,
):
    x, yh, z, yl, p = place()
    b = z % 2
    xu, xd, xo = (x + 1) % 4, (x + 3) % 4, (x + 2) % 4
    at_core = device(x, yh, z, yl, 1 - p)
    at_xu, at_xd, at_xo = [device(k, yh, z, yl, p) for k in (xu, xd, xo)]
    y_up, y_dn = (yh * 4 + yl + 1) % 8, (yh * 4 + yl + 7) % 8
    at_yu, at_yd = [device(x, k // 4, z, k % 4, p) for k in (y_up, y_dn)]
    at_zu, at_zd = [device(x, yh, k % 8, yl, p) for k in (z + 1, z + 7)]
    at_y = [device(x, yh, z, (yl + d) % 4, p) for d in (1, 2, 3)]
    cached = cached_ref[0]
    width = kbuf.shape[-1]
    half = 16

    mine = pl.ds(p * half, half)
    local = [
        pltpu.make_async_copy(pool_in, pbuf.at[mine], lsem.at[0]),
        pltpu.make_async_copy(q_in, qbuf.at[0], lsem.at[1]),
        pltpu.make_async_copy(new_in, newt, lsem.at[2]),
    ]
    load_w = pltpu.make_async_copy(w_in, w, lsem.at[3])
    load_uv = pltpu.make_async_copy(w_uv, wt, lsem.at[4])
    for copy in local + [load_uv, load_w]:
        copy.start()
    greet([at_core, at_xu, at_xd, at_xo, at_yu, at_yd, at_zu, at_zd] + at_y)

    push = remote(pool_in, pbuf.at[mine], psem.at[0], psem.at[1], at_core)
    push.start()
    q_up = remote(q_in, qbuf.at[1], qs.at[0], qr.at[0], at_xu)
    q_dn = remote(q_in, qbuf.at[2], qs.at[1], qr.at[1], at_xd)
    q_up.start()
    q_dn.start()
    q_up2 = remote(qbuf.at[1, 0], qbuf.at[3, 0], qs.at[2], qr.at[2], at_xu)
    q_dn2 = remote(qbuf.at[2, 1], qbuf.at[3, 1], qs.at[3], qr.at[3], at_xd)

    for copy in local:
        copy.wait()
    kbuf[0, 32:36] = newt[...].T.reshape(4, UNIT, width)
    push.wait_recv()

    def gather(k, carry):
        kbuf[0, pl.ds(2 * k, 2)] = pbuf[blocks[k]].reshape(2, UNIT, width)
        return carry

    lax.fori_loop(0, half, gather, 0)

    def y_up_copy(s, j):
        u = j * 4 + b * 2
        return remote(kbuf.at[s, u], kbuf.at[1, u], ups.at[j], upr.at[j], at_yu)

    def y_dn_copy(s, j):
        u = j * 4 + b * 2 + 1
        return remote(kbuf.at[s, u], kbuf.at[1, u], dns.at[j], dnr.at[j], at_yd)

    def z_up_copy(j, base):
        u = j * 4 + base * 2
        return remote(kbuf.at[1, u], kbuf.at[1, u], zus.at[j], zur.at[j], at_zu)

    def z_dn_copy(j, base):
        u = j * 4 + base * 2 + 1
        return remote(kbuf.at[1, u], kbuf.at[1, u], zds.at[j], zdr.at[j], at_zd)

    @pl.when(yl == 3)
    def _():
        for j in range(9):
            y_up_copy(0, j).start()

    @pl.when(yl == 0)
    def _():
        for j in range(9):
            y_dn_copy(0, j).start()

    def forward(step):
        j = step - 1 - yl

        @pl.when((j >= 0) & (j < 9))
        def _():
            y_up_copy(1, j).wait_recv()

            @pl.when(yl != 3)
            def _():
                y_up_copy(1, j).start()

            z_up_copy(j, b).start()

        k = step - 4 + yl

        @pl.when((k >= 0) & (k < 9))
        def _():
            y_dn_copy(1, k).wait_recv()

            @pl.when(yl != 0)
            def _():
                y_dn_copy(1, k).start()

            z_dn_copy(k, b).start()

    owners = [x, xd, xu, xo]

    def attend(slots, s_at, tile):
        c = x * 2 + (yh if s_at == 0 else 1 - yh)
        lo, lanes = slots[0] * 256, len(slots) * 256
        cols = slice(lo, lo + lanes)
        units = slice(tile * 12, tile * 12 + 12)
        keys = kbuf[s_at, units].reshape(384, width)
        query = jnp.concatenate([qbuf[g, h] for g in slots for h in range(2)], axis=1)
        s = jnp.dot(keys, query, preferred_element_type=F32) * SCALE
        hist = 384 if tile < 2 else 256
        row = lax.broadcasted_iota(jnp.int32, (hist, lanes), 0)
        s_hist = jnp.where(row < cached - c * 1024 - tile * 384, s[:hist], NEG)
        if tile == 2:
            token = lax.broadcasted_iota(jnp.int32, (1, 256), 1) % 128
            last = jnp.concatenate([token + (owners[g] * 2 + yh - c) * 128 for g in slots], axis=1)
            row = lax.broadcasted_iota(jnp.int32, (128, lanes), 0)
            s = jnp.concatenate([s_hist, jnp.where(row <= last, s[hist:], NEG)], axis=0)
        else:
            s = s_hist
        fresh = s_at == 0 and tile == 0
        top = jnp.max(s, axis=0, keepdims=True)
        if not fresh:
            old = stat[0:1, cols]
            top = jnp.maximum(top, old)
        e = jnp.exp2(s - top)
        total = jnp.sum(e, axis=0, keepdims=True)
        o = jnp.dot(vt[s_at, :, tile * 384:(tile + 1) * 384], e.astype(BF16), preferred_element_type=F32)
        if not fresh:
            f = jnp.exp2(old - top)
            total = total + f * stat[1:2, cols]
            o = o + f * acc[:, cols]
        stat[0:1, cols] = top
        stat[1:2, cols] = total
        acc[:, cols] = o

    def turn(s_at, tile):
        v = kbuf[s_at, tile * 12:tile * 12 + 12].reshape(384, width)[:, :LAT]
        vt[s_at, :, tile * 384:(tile + 1) * 384] = v.T

    def turn_w(i):
        wo[i * 896:(i + 1) * 896] = w[:, i * 896:(i + 1) * 896].T

    near, far = (0, 1), (2, 3)
    for t in range(3):
        turn(0, t)
    forward(1)
    load_w.wait()
    turn_w(0)
    forward(2)
    q_up.wait_recv()
    q_up2.start()
    q_dn.wait_recv()
    q_dn2.start()
    forward(3)
    attend(near, 0, 0)
    forward(4)
    attend(near, 0, 1)
    forward(5)
    attend(near, 0, 2)
    forward(6)
    q_up2.wait_recv()
    q_dn2.wait_recv()
    attend(far, 0, 0)
    forward(7)
    attend(far, 0, 1)
    forward(8)
    attend(far, 0, 2)
    forward(9)
    turn_w(1)
    load_uv.wait()

    def landed(tile):
        for j in range(3 * tile, 3 * tile + 3):
            z_up_copy(j, 1 - b).wait_recv()
            z_dn_copy(j, 1 - b).wait_recv()
        turn(1, tile)

    landed(0)
    attend(near, 1, 0)
    forward(10)
    attend(far, 1, 0)
    forward(11)
    turn_w(2)
    turn_w(3)
    forward(12)
    landed(1)
    attend(near, 1, 1)
    attend(far, 1, 1)
    for i in range(4, 8):
        turn_w(i)
    landed(2)

    results = []
    for slots in (far, near):
        attend(slots, 1, 2)
        for g in reversed(slots):
            cols = slice(g * 256, (g + 1) * 256)
            lat = (acc[:, cols] / stat[1:2, cols]).astype(BF16)
            for h in range(2):
                o = lax.dot_general(
                    wt[h], lat[:, h * 128:(h + 1) * 128], (((0,), (0,)), ((), ())), preferred_element_type=F32
                )
                ores[g, :, h * 128:(h + 1) * 128] = o.astype(BF16)
            if g:
                sstat[g - 1, 0:2] = stat[0:2, cols]
                to = {1: at_xd, 2: at_xu, 3: at_xo}[g]
                sent = [
                    remote(ores.at[g], orecv.at[g - 1], os_.at[g - 1], or_.at[g - 1], to),
                    remote(sstat.at[g - 1], srecv.at[g - 1], ss.at[g - 1], sr.at[g - 1], to),
                ]
                for copy in sent:
                    copy.start()
                results += sent

    for copy in results:
        copy.wait_recv()
    tops = [stat[0:1, 0:256]] + [srecv[i, 0:1] for i in range(3)]
    sums = [stat[1:2, 0:256]] + [srecv[i, 1:2] for i in range(3)]
    outs = [ores[0]] + [orecv[i] for i in range(3)]
    top = jnp.maximum(jnp.maximum(tops[0], tops[1]), jnp.maximum(tops[2], tops[3]))
    shares = [t * jnp.exp2(m - top) for m, t in zip(tops, sums)]
    inv = 1.0 / (shares[0] + shares[1] + shares[2] + shares[3])
    head = sum(o.astype(F32) * (s * inv) for o, s in zip(outs, shares))
    for h in range(2):
        at[h * 128:(h + 1) * 128] = head[:, h * 128:(h + 1) * 128].astype(BF16)

    a = at[...]

    def term(dest, d):
        row = pl.multiple_of((dest % 8) * 896 + ((yl + 1 + d) % 4) * 224, 16)
        return jnp.dot(wo[pl.ds(row, 224)], a, preferred_element_type=F32)

    def up(s, d):
        return remote(up_out.at[s, d], up_in.at[s, d], us.at[s, d], ur.at[s, d], at_zu)

    def dn(s, d):
        return remote(dn_out.at[s, d], dn_in.at[s, d], ds.at[s, d], dr.at[s, d], at_zd)

    started = []
    for s in range(4):
        for d in range(4):
            for flow, dest, sent, got, extra in (
                (up, z + 4 - s, up_out, up_in, (2, 3)),
                (dn, z + 4 + s, dn_out, dn_in, (0, 1)),
            ):
                if s == 0 and d not in extra:
                    continue
                v = term(dest, d)
                if s > 1 or (s == 1 and d in extra):
                    flow(s - 1, d).wait_recv()
                    v = v + got[s - 1, d].astype(F32)
                sent[s, d] = v.astype(BF16)
                started.append(flow(s, d))
                started[-1].start()

    for d in range(4):
        v = term(z, d)
        up(3, d).wait_recv()
        dn(3, d).wait_recv()
        v = v + up_in[3, d].astype(F32) + dn_in[3, d].astype(F32)
        if d < 3:
            y_out[d] = v.astype(BF16)
            copy = remote(y_out.at[d], y_in.at[d], ys.at[d], yr.at[d], at_y[d])
            copy.start()
            started.append(copy)
        else:
            own[...] = v
    v = own[...]
    for d in range(3):
        started[d - 3].wait_recv()
        v = v + y_in[d].astype(F32)
    out[...] = v.astype(BF16)

    push.wait_send()
    for copy in (q_up, q_dn, q_up2, q_dn2):
        copy.wait_send()
    for j in range(9):
        y_up_copy(1, j).wait_send()
        y_dn_copy(1, j).wait_send()
        z_up_copy(j, b).wait_send()
        z_dn_copy(j, b).wait_send()
    for copy in results + started:
        copy.wait_send()


def body(queries, new_latent, cache_pool, block_list, cached_lengths, w_uv, w_o):
    width = queries.shape[-1]
    columns = w_o.shape[-1]
    q = jnp.transpose(queries[0], (1, 2, 0))
    new = new_latent[0].T
    hbm = pl.BlockSpec(memory_space=pltpu.HBM)
    smem = pl.BlockSpec(memory_space=pltpu.SMEM)
    dma = pltpu.SemaphoreType.DMA
    mixed = pl.pallas_call(
        kernel,
        out_shape=jax.ShapeDtypeStruct((224, 128), BF16),
        in_specs=[smem, smem, hbm, hbm, hbm, hbm, hbm],
        out_specs=pl.BlockSpec(memory_space=pltpu.VMEM),
        scratch_shapes=[
            pltpu.VMEM((4, 2, width, 128), BF16),
            pltpu.VMEM((32, 64, width), BF16),
            pltpu.VMEM((2, 36, UNIT, width), BF16),
            pltpu.VMEM((width, 128), BF16),
            pltpu.VMEM((2, LAT, 36 * UNIT), BF16),
            pltpu.VMEM((2, LAT, VH), BF16),
            pltpu.VMEM((LAT, 1024), F32),
            pltpu.VMEM((8, 1024), F32),
            pltpu.VMEM((4, VH, 256), BF16),
            pltpu.VMEM((3, VH, 256), BF16),
            pltpu.VMEM((3, 8, 256), F32),
            pltpu.VMEM((3, 8, 256), F32),
            pltpu.VMEM((256, columns), BF16),
            pltpu.VMEM((columns, 256), BF16),
            pltpu.VMEM((256, 128), BF16),
            pltpu.VMEM((4, 4, 224, 128), BF16),
            pltpu.VMEM((4, 4, 224, 128), BF16),
            pltpu.VMEM((4, 4, 224, 128), BF16),
            pltpu.VMEM((4, 4, 224, 128), BF16),
            pltpu.VMEM((224, 128), F32),
            pltpu.VMEM((3, 224, 128), BF16),
            pltpu.VMEM((3, 224, 128), BF16),
            dma((5,)), dma((2,)), dma((4,)), dma((4,)),
            dma((9,)), dma((9,)), dma((9,)), dma((9,)),
            dma((9,)), dma((9,)), dma((9,)), dma((9,)),
            dma((3,)), dma((3,)), dma((3,)), dma((3,)),
            dma((4, 4)), dma((4, 4)), dma((4, 4)), dma((4, 4)), dma((3,)), dma((3,)),
        ],
        compiler_params=pltpu.CompilerParams(
            collective_id=0, has_side_effects=True, vmem_limit_bytes=56 * 2**20
        ),
        cost_estimate=pl.CostEstimate(flops=6 * 10**9, bytes_accessed=8 * 10**6, transcendentals=2 * 10**6),
    )(block_list[0, 0], cached_lengths, q, new, cache_pool[0], w_uv, w_o.reshape(256, columns))
    return mixed.T[None]


def solution(mesh):
    in_specs = (
        P("pool", "ctx", "head", None),
        P("pool", "ctx", None),
        P("ctx", "pool", None, None),
        P("pool", "ctx", None),
        P("pool"),
        P("head", None, None),
        P("head", None, None),
    )
    out_specs = P("pool", "ctx", "head")
    return jax.shard_map(body, mesh=mesh, in_specs=in_specs, out_specs=out_specs, check_vma=False)
```

```python
import jax
import jax.numpy as jnp
from jax import lax
from jax.experimental import pallas as pl
from jax.experimental.pallas import tpu as pltpu
from jax.sharding import PartitionSpec as P

MESH = pl.DeviceIdType.MESH
LAT = 512
VH = 128
UNIT = 32
HOP = 4
SCALE = 192.0 ** -0.5 * 1.4426950408889634
NEG = -1e30
F32 = jnp.float32
BF16 = jnp.bfloat16


def place():
    c, h, p = lax.axis_index("ctx"), lax.axis_index("head"), lax.axis_index("pool")
    return c // 2, c % 2, h // 4, h % 4, p


def device(x, yh, z, yl, p):
    return {"ctx": x * 2 + yh, "head": z * 4 + yl, "pool": p}


def greet(others):
    barrier = pltpu.get_barrier_semaphore()
    for other in others:
        pl.semaphore_signal(barrier, inc=1, device_id=other, device_id_type=MESH)
    pl.semaphore_wait(barrier, len(others))


def remote(src, dst, send, recv, to):
    return pltpu.make_async_remote_copy(
        src_ref=src, dst_ref=dst, send_sem=send, recv_sem=recv, device_id=to, device_id_type=MESH
    )


def kernel(
    blocks, cached_ref, q_in, new_in, pool_in, w_uv, w_in,
    out,
    qbuf, pbuf, kbuf, newt, vt, wt, acc, stat, ores, orecv, sstat, srecv,
    w, wo, at, up_out, up_in, dn_out, dn_in, own, y_out, y_in,
    lsem, psem, qs, qr, ups, upr, dns, dnr, zus, zur, zds, zdr, os_, or_, ss, sr,
    us, ur, ds, dr, ys, yr,
):
    x, yh, z, yl, p = place()
    b = z % 2
    xu, xd, xo = (x + 1) % 4, (x + 3) % 4, (x + 2) % 4
    at_core = device(x, yh, z, yl, 1 - p)
    at_xu, at_xd, at_xo = [device(k, yh, z, yl, p) for k in (xu, xd, xo)]
    y_up, y_dn = (yh * 4 + yl + 1) % 8, (yh * 4 + yl + 7) % 8
    at_yu, at_yd = [device(x, k // 4, z, k % 4, p) for k in (y_up, y_dn)]
    at_zu, at_zd = [device(x, yh, k % 8, yl, p) for k in (z + 1, z + 7)]
    at_y = [device(x, yh, z, (yl + d) % 4, p) for d in (1, 2, 3)]
    cached = cached_ref[0]
    width = q_in.shape[1]
    half = 16

    mine = pl.ds(p * half, half)
    local = [
        pltpu.make_async_copy(pool_in, pbuf.at[mine], lsem.at[0]),
        pltpu.make_async_copy(q_in, qbuf.at[0], lsem.at[1]),
        pltpu.make_async_copy(new_in, newt, lsem.at[2]),
    ]
    load_w = pltpu.make_async_copy(w_in, w, lsem.at[3])
    load_uv = pltpu.make_async_copy(w_uv, wt, lsem.at[4])
    for copy in local + [load_uv, load_w]:
        copy.start()
    greet([at_core, at_xu, at_xd, at_xo, at_yu, at_yd, at_zu, at_zd] + at_y)

    push = remote(pool_in, pbuf.at[mine], psem.at[0], psem.at[1], at_core)
    push.start()
    q_up = [remote(q_in.at[h], qbuf.at[1, h], qs.at[h], qr.at[h], at_xu) for h in range(2)]
    q_dn = [remote(q_in.at[h], qbuf.at[2, h], qs.at[2 + h], qr.at[2 + h], at_xd) for h in range(2)]
    for copy in (q_up[0], q_dn[1], q_up[1], q_dn[0]):
        copy.start()
    q_up2 = remote(qbuf.at[1, 0], qbuf.at[3, 0], qs.at[4], qr.at[4], at_xu)
    q_dn2 = remote(qbuf.at[2, 1], qbuf.at[3, 1], qs.at[5], qr.at[5], at_xd)

    for copy in local:
        copy.wait()
    kbuf[0, :, :, width:] = jnp.zeros((36, UNIT, kbuf.shape[-1] - width), BF16)
    kbuf[0, 0:4, :, :width] = newt[...].T.reshape(4, UNIT, width)

    def y_up_copy(s, j):
        u = j * 4 + b * 2
        return remote(kbuf.at[s, u], kbuf.at[1, u], ups.at[j], upr.at[j], at_yu)

    def y_dn_copy(s, j):
        u = j * 4 + b * 2 + 1
        return remote(kbuf.at[s, u], kbuf.at[1, u], dns.at[j], dnr.at[j], at_yd)

    def z_up_copy(j, base):
        u = j * 4 + base * 2
        return remote(kbuf.at[1, u], kbuf.at[1, u], zus.at[j], zur.at[j], at_zu)

    def z_dn_copy(j, base):
        u = j * 4 + base * 2 + 1
        return remote(kbuf.at[1, u], kbuf.at[1, u], zds.at[j], zdr.at[j], at_zd)

    def first(lo, hi):
        @pl.when(yl == 3)
        def _():
            for j in range(lo, hi):
                y_up_copy(0, j).start()

        @pl.when(yl == 0)
        def _():
            for j in range(lo, hi):
                y_dn_copy(0, j).start()

    first(0, 1)
    push.wait_recv()

    def gather(k, carry):
        kbuf[0, pl.ds(2 * k + 4, 2), :, :width] = pbuf[blocks[k]].reshape(2, UNIT, width)
        return carry

    lax.fori_loop(0, half, gather, 0)
    first(1, 9)

    def forward(step):
        j = step - HOP * (yl + 1)

        @pl.when((j >= 0) & (j < 9))
        def _():
            y_up_copy(1, j).wait_recv()

            @pl.when(yl != 3)
            def _():
                y_up_copy(1, j).start()

            z_up_copy(j, b).start()

        k = step - HOP * (4 - yl)

        @pl.when((k >= 0) & (k < 9))
        def _():
            y_dn_copy(1, k).wait_recv()

            @pl.when(yl != 0)
            def _():
                y_dn_copy(1, k).start()

            z_dn_copy(k, b).start()

    owners = [x, xd, xu, xo]

    def attend(slots, s_at, tile):
        c = x * 2 + (yh if s_at == 0 else 1 - yh)
        lo, lanes = slots[0] * 256, len(slots) * 256
        cols = slice(lo, lo + lanes)
        units = slice(tile * 12, tile * 12 + 12)
        keys = kbuf[s_at, units].reshape(384, kbuf.shape[-1])[:, :width]
        query = jnp.concatenate([qbuf[g, h] for g in slots for h in range(2)], axis=1)
        s = jnp.dot(keys, query, preferred_element_type=F32) * SCALE
        new = 0 if tile else 128
        row = lax.broadcasted_iota(jnp.int32, (384 - new, lanes), 0)
        s_hist = jnp.where(row < cached - c * 1024 - (tile * 384 + new - 128), s[new:], NEG)
        if new:
            token = lax.broadcasted_iota(jnp.int32, (1, 256), 1) % 128
            last = jnp.concatenate([token + (owners[g] * 2 + yh - c) * 128 for g in slots], axis=1)
            row = lax.broadcasted_iota(jnp.int32, (128, lanes), 0)
            s = jnp.concatenate([jnp.where(row <= last, s[:new], NEG), s_hist], axis=0)
        else:
            s = s_hist
        fresh = s_at == 0 and tile == 0
        top = jnp.max(s, axis=0, keepdims=True)
        if not fresh:
            old = stat[0:1, cols]
            top = jnp.maximum(top, old)
        e = jnp.exp2(s - top)
        total = jnp.sum(e, axis=0, keepdims=True)
        o = jnp.dot(vt[s_at, :, tile * 384:(tile + 1) * 384], e.astype(BF16), preferred_element_type=F32)
        if not fresh:
            f = jnp.exp2(old - top)
            total = total + f * stat[1:2, cols]
            o = o + f * acc[:, cols]
        stat[0:1, cols] = top
        stat[1:2, cols] = total
        acc[:, cols] = o

    def turn(s_at, tile):
        v = kbuf[s_at, tile * 12:tile * 12 + 12].reshape(384, kbuf.shape[-1])[:, :LAT]
        vt[s_at, :, tile * 384:(tile + 1) * 384] = v.T

    def turn_w(i):
        wo[i * 896:(i + 1) * 896] = w[:, i * 896:(i + 1) * 896].T

    near, far = (0, 1), (2, 3)
    for t in range(3):
        turn(0, t)
    q_up[0].wait_recv()
    q_up2.start()
    q_dn[1].wait_recv()
    q_dn2.start()
    load_w.wait()
    forward(4)
    turn_w(0)
    forward(5)
    turn_w(1)
    forward(6)
    q_up[1].wait_recv()
    attend(near, 0, 0)
    forward(7)
    attend(near, 0, 1)
    forward(8)
    attend(near, 0, 2)
    forward(9)
    turn_w(2)
    forward(10)
    q_dn[0].wait_recv()
    q_up2.wait_recv()
    q_dn2.wait_recv()
    attend(far, 0, 0)
    forward(11)
    attend(far, 0, 1)
    forward(12)
    attend(far, 0, 2)
    forward(13)
    load_uv.wait()
    for step in range(14, 25):
        if step % 2 == 0 and step < 24:
            turn_w(step // 2 - 4)
        forward(step)

    def landed(tile):
        for j in range(3 * tile, 3 * tile + 3):
            z_up_copy(j, 1 - b).wait_recv()
            z_dn_copy(j, 1 - b).wait_recv()
        turn(1, tile)

    landed(0)
    attend(near, 1, 0)
    attend(far, 1, 0)
    landed(1)
    attend(near, 1, 1)
    attend(far, 1, 1)
    landed(2)

    results = []
    for slots in (far, near):
        attend(slots, 1, 2)
        for g in reversed(slots):
            cols = slice(g * 256, (g + 1) * 256)
            lat = (acc[:, cols] / stat[1:2, cols]).astype(BF16)
            for h in range(2):
                o = lax.dot_general(
                    wt[h], lat[:, h * 128:(h + 1) * 128], (((0,), (0,)), ((), ())), preferred_element_type=F32
                )
                ores[g, :, h * 128:(h + 1) * 128] = o.astype(BF16)
            if g:
                sstat[g - 1, 0:2] = stat[0:2, cols]
                to = {1: at_xd, 2: at_xu, 3: at_xo}[g]
                sent = [
                    remote(ores.at[g], orecv.at[g - 1], os_.at[g - 1], or_.at[g - 1], to),
                    remote(sstat.at[g - 1], srecv.at[g - 1], ss.at[g - 1], sr.at[g - 1], to),
                ]
                for copy in sent:
                    copy.start()
                results += sent

    for copy in results:
        copy.wait_recv()
    tops = [stat[0:1, 0:256]] + [srecv[i, 0:1] for i in range(3)]
    sums = [stat[1:2, 0:256]] + [srecv[i, 1:2] for i in range(3)]
    outs = [ores[0]] + [orecv[i] for i in range(3)]
    top = jnp.maximum(jnp.maximum(tops[0], tops[1]), jnp.maximum(tops[2], tops[3]))
    shares = [t * jnp.exp2(m - top) for m, t in zip(tops, sums)]
    inv = 1.0 / (shares[0] + shares[1] + shares[2] + shares[3])
    head = sum(o.astype(F32) * (s * inv) for o, s in zip(outs, shares))
    for h in range(2):
        at[h * 128:(h + 1) * 128] = head[:, h * 128:(h + 1) * 128].astype(BF16)

    a = at[...]

    def term(dest, d):
        row = pl.multiple_of((dest % 8) * 896 + ((yl + 1 + d) % 4) * 224, 16)
        return jnp.dot(wo[pl.ds(row, 224)], a, preferred_element_type=F32)

    def up(s, d):
        return remote(up_out.at[s, d], up_in.at[s, d], us.at[s, d], ur.at[s, d], at_zu)

    def dn(s, d):
        return remote(dn_out.at[s, d], dn_in.at[s, d], ds.at[s, d], dr.at[s, d], at_zd)

    started = []
    for s in range(4):
        for d in range(4):
            for flow, dest, sent, got, extra in (
                (up, z + 4 - s, up_out, up_in, (2, 3)),
                (dn, z + 4 + s, dn_out, dn_in, (0, 1)),
            ):
                if s == 0 and d not in extra:
                    continue
                v = term(dest, d)
                if s > 1 or (s == 1 and d in extra):
                    flow(s - 1, d).wait_recv()
                    v = v + got[s - 1, d].astype(F32)
                sent[s, d] = v.astype(BF16)
                started.append(flow(s, d))
                started[-1].start()

    for d in range(4):
        v = term(z, d)
        up(3, d).wait_recv()
        dn(3, d).wait_recv()
        v = v + up_in[3, d].astype(F32) + dn_in[3, d].astype(F32)
        if d < 3:
            y_out[d] = v.astype(BF16)
            copy = remote(y_out.at[d], y_in.at[d], ys.at[d], yr.at[d], at_y[d])
            copy.start()
            started.append(copy)
        else:
            own[...] = v
    v = own[...]
    for d in range(3):
        started[d - 3].wait_recv()
        v = v + y_in[d].astype(F32)
    out[...] = v.astype(BF16)

    push.wait_send()
    for copy in q_up + q_dn + [q_up2, q_dn2]:
        copy.wait_send()
    for j in range(9):
        y_up_copy(1, j).wait_send()
        y_dn_copy(1, j).wait_send()
        z_up_copy(j, b).wait_send()
        z_dn_copy(j, b).wait_send()
    for copy in results + started:
        copy.wait_send()


def body(queries, new_latent, cache_pool, block_list, cached_lengths, w_uv, w_o):
    width = queries.shape[-1]
    columns = w_o.shape[-1]
    q = jnp.transpose(queries[0], (1, 2, 0))
    new = new_latent[0].T
    hbm = pl.BlockSpec(memory_space=pltpu.HBM)
    smem = pl.BlockSpec(memory_space=pltpu.SMEM)
    dma = pltpu.SemaphoreType.DMA
    mixed = pl.pallas_call(
        kernel,
        out_shape=jax.ShapeDtypeStruct((224, 128), BF16),
        in_specs=[smem, smem, hbm, hbm, hbm, hbm, hbm],
        out_specs=pl.BlockSpec(memory_space=pltpu.VMEM),
        scratch_shapes=[
            pltpu.VMEM((4, 2, width, 128), BF16),
            pltpu.VMEM((32, 64, width), BF16),
            pltpu.VMEM((2, 36, UNIT, 640), BF16),
            pltpu.VMEM((width, 128), BF16),
            pltpu.VMEM((2, LAT, 36 * UNIT), BF16),
            pltpu.VMEM((2, LAT, VH), BF16),
            pltpu.VMEM((LAT, 1024), F32),
            pltpu.VMEM((8, 1024), F32),
            pltpu.VMEM((4, VH, 256), BF16),
            pltpu.VMEM((3, VH, 256), BF16),
            pltpu.VMEM((3, 8, 256), F32),
            pltpu.VMEM((3, 8, 256), F32),
            pltpu.VMEM((256, columns), BF16),
            pltpu.VMEM((columns, 256), BF16),
            pltpu.VMEM((256, 128), BF16),
            pltpu.VMEM((4, 4, 224, 128), BF16),
            pltpu.VMEM((4, 4, 224, 128), BF16),
            pltpu.VMEM((4, 4, 224, 128), BF16),
            pltpu.VMEM((4, 4, 224, 128), BF16),
            pltpu.VMEM((224, 128), F32),
            pltpu.VMEM((3, 224, 128), BF16),
            pltpu.VMEM((3, 224, 128), BF16),
            dma((5,)), dma((2,)), dma((6,)), dma((6,)),
            dma((9,)), dma((9,)), dma((9,)), dma((9,)),
            dma((9,)), dma((9,)), dma((9,)), dma((9,)),
            dma((3,)), dma((3,)), dma((3,)), dma((3,)),
            dma((4, 4)), dma((4, 4)), dma((4, 4)), dma((4, 4)), dma((3,)), dma((3,)),
        ],
        compiler_params=pltpu.CompilerParams(
            collective_id=0, has_side_effects=True, vmem_limit_bytes=56 * 2**20
        ),
        cost_estimate=pl.CostEstimate(flops=6 * 10**9, bytes_accessed=8 * 10**6, transcendentals=2 * 10**6),
    )(block_list[0, 0], cached_lengths, q, new, cache_pool[0], w_uv, w_o.reshape(256, columns))
    return mixed.T[None]


def solution(mesh):
    in_specs = (
        P("pool", "ctx", "head", None),
        P("pool", "ctx", None),
        P("ctx", "pool", None, None),
        P("pool", "ctx", None),
        P("pool"),
        P("head", None, None),
        P("head", None, None),
    )
    out_specs = P("pool", "ctx", "head")
    return jax.shard_map(body, mesh=mesh, in_specs=in_specs, out_specs=out_specs, check_vma=False)
```

```python
import jax
import jax.numpy as jnp
from jax import lax
from jax.experimental import pallas as pl
from jax.experimental.pallas import tpu as pltpu
from jax.sharding import PartitionSpec as P

MESH = pl.DeviceIdType.MESH
LAT = 512
VH = 128
UNIT = 32
UNITS = 1152 // UNIT
NEW_UNITS = 128 // UNIT
TURNS = UNITS // 4
HOP = 4
TILES = ((0, 384), (384, 896), (896, 1152))
SCALE = 192.0 ** -0.5 * 1.4426950408889634
NEG = -1e30
ZF, YF = 144, 80
Z_ORDER = (4, 3, 5, 2, 6, 1, 7, 0)
Z_GROUPS = ((0, 1), (1, 3), (3, 5), (5, 7), (7, 8))
F32 = jnp.float32
BF16 = jnp.bfloat16


def place():
    c, h, p = lax.axis_index("ctx"), lax.axis_index("head"), lax.axis_index("pool")
    return c // 2, c % 2, h // 4, h % 4, p


def device(x, yh, z, yl, p):
    return {"ctx": x * 2 + yh, "head": z * 4 + yl, "pool": p}


def greet(others):
    barrier = pltpu.get_barrier_semaphore()
    for other in others:
        pl.semaphore_signal(barrier, inc=1, device_id=other, device_id_type=MESH)
    pl.semaphore_wait(barrier, len(others))


def remote(src, dst, send, recv, to):
    return pltpu.make_async_remote_copy(
        src_ref=src, dst_ref=dst, send_sem=send, recv_sem=recv, device_id=to, device_id_type=MESH
    )


def kernel(
    blocks, cached_ref, q_in, new_in, pool_in, w_uv, w_in,
    out,
    qbuf, pbuf0, pbuf1, kbuf, newt, vt, wt, acc, stat, ores, orecv, sstat, srecv,
    w, wo, at, up_out, up_in, dn_out, dn_in, own, y_out, y_in, yf_out, yf_in, zf_out, zf_in,
    lsem, psem, qs, qr, ks, kr, os_, or_, ss, sr,
    us, ur, ds, dr, ys, yr, yfs, yfr, zfs, zfr,
):
    x, yh, z, yl, p = place()
    b = z % 2
    xu, xd, xo = (x + 1) % 4, (x + 3) % 4, (x + 2) % 4
    at_core = device(x, yh, z, yl, 1 - p)
    at_xu, at_xd, at_xo = [device(k, yh, z, yl, p) for k in (xu, xd, xo)]
    y_up, y_dn = (yh * 4 + yl + 1) % 8, (yh * 4 + yl + 7) % 8
    at_yu, at_yd = [device(x, k // 4, z, k % 4, p) for k in (y_up, y_dn)]
    at_z = [device(x, yh, (z + k) % 8, yl, p) for k in range(1, 8)]
    at_zu, at_zd = at_z[0], at_z[6]
    at_y = [device(x, yh, z, (yl + d) % 4, p) for d in (1, 2, 3)]
    cached = cached_ref[0]
    width = q_in.shape[1]
    half = 16

    mine = pl.ds(p * half, half)
    local = [
        pltpu.make_async_copy(pool_in.at[:, pl.ds(0, 32)], pbuf0.at[mine], lsem.at[0]),
        pltpu.make_async_copy(pool_in.at[:, pl.ds(32, 32)], pbuf1.at[mine], lsem.at[5]),
        pltpu.make_async_copy(q_in, qbuf.at[0], lsem.at[1]),
        pltpu.make_async_copy(new_in, newt, lsem.at[2]),
    ]
    load_w = pltpu.make_async_copy(w_in, w, lsem.at[3])
    load_uv = pltpu.make_async_copy(w_uv, wt, lsem.at[4])
    for copy in local + [load_uv, load_w]:
        copy.start()
    greet([at_core, at_xu, at_xd, at_xo, at_yu, at_yd] + at_z + at_y)

    push = []
    for i, pbuf in enumerate((pbuf0, pbuf1)):
        rows = pl.ds(i * 32, 32)
        push.append(remote(pool_in.at[:, rows], pbuf.at[mine], psem.at[i], psem.at[2 + i], at_core))
        push[i].start()
    q_up = [remote(q_in.at[h], qbuf.at[1, h], qs, qr.at[h], at_xu) for h in range(2)]
    q_dn = [remote(q_in.at[h], qbuf.at[2, h], qs, qr.at[2 + h], at_xd) for h in range(2)]
    for copy in (q_up[0], q_dn[1], q_up[1], q_dn[0]):
        copy.start()
    q_up2 = remote(qbuf.at[1, 0], qbuf.at[3, 0], qs, qr.at[4], at_xu)
    q_dn2 = remote(qbuf.at[2, 1], qbuf.at[3, 1], qs, qr.at[5], at_xd)

    for copy in local:
        copy.wait()
    kbuf[0, :, :, width:] = jnp.zeros((UNITS, UNIT, kbuf.shape[-1] - width), BF16)
    kbuf[0, 0:NEW_UNITS, :, :width] = newt[...].T.reshape(NEW_UNITS, UNIT, width)

    def y_up_copy(s, j):
        u = j * 4 + b * 2
        return remote(kbuf.at[s, u], kbuf.at[1, u], ks, kr.at[0, j], at_yu)

    def y_dn_copy(s, j):
        u = j * 4 + b * 2 + 1
        return remote(kbuf.at[s, u], kbuf.at[1, u], ks, kr.at[1, j], at_yd)

    def z_up_copy(j, base):
        u = j * 4 + base * 2
        return remote(kbuf.at[1, u], kbuf.at[1, u], ks, kr.at[2, j], at_zu)

    def z_dn_copy(j, base):
        u = j * 4 + base * 2 + 1
        return remote(kbuf.at[1, u], kbuf.at[1, u], ks, kr.at[3, j], at_zd)

    def first(lo, hi):
        @pl.when(yl == 3)
        def _():
            for j in range(lo, hi):
                y_up_copy(0, j).start()

        @pl.when(yl == 0)
        def _():
            for j in range(lo, hi):
                y_dn_copy(0, j).start()

    first(0, NEW_UNITS // 4)
    per_half = half * 32 // UNIT
    for i, pbuf in enumerate((pbuf0, pbuf1)):
        push[i].wait_recv()

        def gather(k, carry):
            u = NEW_UNITS + i * per_half + k * (32 // UNIT)
            kbuf[0, pl.ds(u, 32 // UNIT), :, :width] = pbuf[blocks[k]].reshape(32 // UNIT, UNIT, width)
            return carry

        lax.fori_loop(0, half, gather, 0)
        first((NEW_UNITS + i * per_half) // 4, (NEW_UNITS + (i + 1) * per_half) // 4)

    def forward(step):
        j = step - HOP * (yl + 1)

        @pl.when((j >= 0) & (j < TURNS))
        def _():
            y_up_copy(1, j).wait_recv()

            @pl.when(yl != 3)
            def _():
                y_up_copy(1, j).start()

            z_up_copy(j, b).start()

        k = step - HOP * (4 - yl)

        @pl.when((k >= 0) & (k < TURNS))
        def _():
            y_dn_copy(1, k).wait_recv()

            @pl.when(yl != 0)
            def _():
                y_dn_copy(1, k).start()

            z_dn_copy(k, b).start()

    owners = [x, xd, xu, xo]

    def attend(slots, s_at, tile):
        c = x * 2 + (yh if s_at == 0 else 1 - yh)
        lo, lanes = slots[0] * 256, len(slots) * 256
        cols = slice(lo, lo + lanes)
        begin, end = TILES[tile]
        rows = end - begin
        keys = kbuf[s_at, begin // UNIT:end // UNIT].reshape(rows, kbuf.shape[-1])[:, :width]
        query = jnp.concatenate([qbuf[g, h] for g in slots for h in range(2)], axis=1)
        s = jnp.dot(keys, query, preferred_element_type=F32) * SCALE
        new = 0 if tile else 128
        row = lax.broadcasted_iota(jnp.int32, (rows - new, lanes), 0) + (begin + new - 128)
        row = ((row >> 5) & 15) * 64 + (row >> 9) * 32 + (row & 31)
        s_hist = jnp.where(row < cached - c * 1024, s[new:], NEG)
        if new:
            token = lax.broadcasted_iota(jnp.int32, (1, 256), 1) % 128
            last = jnp.concatenate([token + (owners[g] * 2 + yh - c) * 128 for g in slots], axis=1)
            row = lax.broadcasted_iota(jnp.int32, (128, lanes), 0)
            s = jnp.concatenate([jnp.where(row <= last, s[:new], NEG), s_hist], axis=0)
        else:
            s = s_hist
        fresh = s_at == 0 and tile == 0
        top = jnp.max(s, axis=0, keepdims=True)
        if not fresh:
            old = stat[0:1, cols]
            top = jnp.maximum(top, old)
        e = jnp.exp2(s - top)
        total = jnp.sum(e, axis=0, keepdims=True)
        o = jnp.dot(vt[s_at, :, begin:end], e.astype(BF16), preferred_element_type=F32)
        if not fresh:
            f = jnp.exp2(old - top)
            total = total + f * stat[1:2, cols]
            o = o + f * acc[:, cols]
        stat[0:1, cols] = top
        stat[1:2, cols] = total
        acc[:, cols] = o

    def turn(s_at, tile):
        begin, end = TILES[tile]
        v = kbuf[s_at, begin // UNIT:end // UNIT].reshape(end - begin, kbuf.shape[-1])[:, :LAT]
        vt[s_at, :, begin:end] = v.T

    def turn_w(i):
        wo[i * 896:(i + 1) * 896] = w[:, i * 896:(i + 1) * 896].T

    near, far = (0, 1), (2, 3)
    for t in range(3):
        turn(0, t)
    q_up[0].wait_recv()
    q_up2.start()
    q_dn[1].wait_recv()
    q_dn2.start()
    load_w.wait()
    load_uv.wait()
    for step in range(HOP, 4 * HOP + TURNS):
        forward(step)
        if step == round(6 * HOP / 4):
            q_up[1].wait_recv()
        if step == round(10 * HOP / 4):
            q_dn[0].wait_recv()
            q_up2.wait_recv()
            q_dn2.wait_recv()
        for t in range(3):
            if step == round((6 + t) * HOP / 4):
                attend(near, 0, t)
            if step == round((10 + t) * HOP / 4):
                attend(far, 0, t)
        for t in range(8):
            if step == round((4 + t if t < 2 else 11 + t) * HOP / 4):
                turn_w(t)

    def landed(tile):
        begin, end = TILES[tile]
        for j in range(begin // UNIT // 4, end // UNIT // 4):
            z_up_copy(j, 1 - b).wait_recv()
            z_dn_copy(j, 1 - b).wait_recv()
        turn(1, tile)

    landed(0)
    attend(near, 1, 0)
    attend(far, 1, 0)
    landed(1)
    attend(near, 1, 1)
    attend(far, 1, 1)
    landed(2)

    results = []
    for slots in (far, near):
        attend(slots, 1, 2)
        for g in reversed(slots):
            cols = slice(g * 256, (g + 1) * 256)
            lat = (acc[:, cols] / stat[1:2, cols]).astype(BF16)
            for h in range(2):
                o = lax.dot_general(
                    wt[h], lat[:, h * 128:(h + 1) * 128], (((0,), (0,)), ((), ())), preferred_element_type=F32
                )
                ores[g, :, h * 128:(h + 1) * 128] = o.astype(BF16)
            if g:
                sstat[g - 1, 0:2] = stat[0:2, cols]
                to = {1: at_xd, 2: at_xu, 3: at_xo}[g]
                sent = [
                    remote(ores.at[g], orecv.at[g - 1], os_, or_.at[g - 1], to),
                    remote(sstat.at[g - 1], srecv.at[g - 1], ss, sr.at[g - 1], to),
                ]
                for copy in sent:
                    copy.start()
                results += sent

    for copy in results:
        copy.wait_recv()
    tops = [stat[0:1, 0:256]] + [srecv[i, 0:1] for i in range(3)]
    sums = [stat[1:2, 0:256]] + [srecv[i, 1:2] for i in range(3)]
    outs = [ores[0]] + [orecv[i] for i in range(3)]
    top = jnp.maximum(jnp.maximum(tops[0], tops[1]), jnp.maximum(tops[2], tops[3]))
    shares = [t * jnp.exp2(m - top) for m, t in zip(tops, sums)]
    inv = 1.0 / (shares[0] + shares[1] + shares[2] + shares[3])
    head = sum(o.astype(F32) * (s * inv) for o, s in zip(outs, shares))
    for h in range(2):
        at[h * 128:(h + 1) * 128] = head[:, h * 128:(h + 1) * 128].astype(BF16)

    a = at[...]

    def term(dest, d, lo, rows):
        row = pl.multiple_of((dest % 8) * 896 + ((yl + 1 + d) % 4) * 224 + lo, 16)
        return jnp.dot(wo[pl.ds(row, rows)], a, preferred_element_type=F32)

    def slot(s, d):
        return s * 4 - 2 + d if s else d % 2

    def flow(way, s, d):
        i = slot(s, d)
        if way == "up":
            return remote(up_out.at[i], up_in.at[i], us, ur.at[i], at_zu)
        return remote(dn_out.at[i], dn_in.at[i], ds, dr.at[i], at_zd)

    def ring(s, order):
        for way, d in order:
            sent, got = (up_out, up_in) if way == "up" else (dn_out, dn_in)
            v = term(z + 4 - s if way == "up" else z + 4 + s, d, 0, ZF)
            if s > 1 or (s == 1 and (d >= 2) == (way == "up")):
                flow(way, s - 1, d).wait_recv()
                v = v + got[slot(s - 1, d)].astype(F32)
            sent[slot(s, d)] = v.astype(BF16)
            flow(way, s, d).start()

    def y_first(g, d):
        lo, hi = Z_GROUPS[g]
        rows = pl.ds(lo, hi - lo)
        return remote(yf_out.at[d, rows], yf_in.at[d, rows], yfs, yfr.at[d, g], at_y[d])

    def send_group(g):
        for d in range(3):
            for i in range(*Z_GROUPS[g]):
                yf_out[d, i] = term(z + Z_ORDER[i], d, ZF, YF).astype(BF16)
            y_first(g, d).start()

    def z_last(i):
        to = device(x, yh, (z + Z_ORDER[i]) % 8, yl, p)
        return remote(zf_out.at[i], zf_in.at[i], zfs, zfr.at[i], to)

    def take_group(g):
        for d in range(3):
            y_first(g, d).wait_recv()
        for i in range(*Z_GROUPS[g]):
            v = term(z + Z_ORDER[i], 3, ZF, YF)
            for d in range(3):
                v = v + yf_in[d, i].astype(F32)
            if Z_ORDER[i]:
                zf_out[i] = v.astype(BF16)
                z_last(i).start()
            else:
                own[ZF:] = v

    def y_last(d):
        return remote(y_out.at[d], y_in.at[d], ys, yr.at[d], at_y[d])

    ring(0, (("up", 2), ("dn", 0), ("up", 3), ("dn", 1)))
    send_group(0)
    ring(1, (("up", 0), ("dn", 2), ("up", 1), ("dn", 3)))
    send_group(1)
    ring(1, (("dn", 0), ("up", 2), ("dn", 1), ("up", 3)))
    send_group(2)
    send_group(3)
    ring(2, (("up", 0), ("dn", 2), ("up", 1), ("dn", 3)))
    take_group(0)
    send_group(4)
    ring(2, (("up", 2), ("dn", 0), ("up", 3), ("dn", 1)))
    take_group(1)
    ring(3, (("up", 0), ("dn", 2), ("up", 1), ("dn", 0)))
    take_group(2)
    ring(3, (("up", 2), ("dn", 1), ("up", 3), ("dn", 3)))
    take_group(3)
    for d in (0, 2, 1, 3):
        v = term(z, d, 0, ZF)
        flow("up", 3, d).wait_recv()
        flow("dn", 3, d).wait_recv()
        i = slot(3, d)
        v = v + up_in[i].astype(F32) + dn_in[i].astype(F32)
        if d < 3:
            y_out[d] = v.astype(BF16)
            y_last(d).start()
        else:
            own[:ZF] = v
    take_group(4)
    v = own[ZF:]
    for i in range(7):
        z_last(i).wait_recv()
        v = v + zf_in[i].astype(F32)
    out[ZF:] = v.astype(BF16)
    v = own[:ZF]
    for d in range(3):
        y_last(d).wait_recv()
        v = v + y_in[d].astype(F32)
    out[:ZF] = v.astype(BF16)

    for copy in push:
        copy.wait_send()
    for ref, sem in (
        (qbuf.at[pl.ds(0, 3)], qs), (kbuf.at[1], ks), (orecv, os_), (srecv, ss), (up_out, us), (dn_out, ds),
        (yf_out, yfs), (zf_out, zfs), (y_out, ys),
    ):
        pltpu.make_async_copy(ref, ref, sem).wait()


def body(queries, new_latent, cache_pool, block_list, cached_lengths, w_uv, w_o):
    width = queries.shape[-1]
    columns = w_o.shape[-1]
    q = jnp.transpose(queries[0], (1, 2, 0))
    new = new_latent[0].T
    hbm = pl.BlockSpec(memory_space=pltpu.HBM)
    smem = pl.BlockSpec(memory_space=pltpu.SMEM)
    dma = pltpu.SemaphoreType.DMA
    mixed = pl.pallas_call(
        kernel,
        out_shape=jax.ShapeDtypeStruct((224, 128), BF16),
        in_specs=[smem, smem, hbm, hbm, hbm, hbm, hbm],
        out_specs=pl.BlockSpec(memory_space=pltpu.VMEM),
        scratch_shapes=[
            pltpu.VMEM((4, 2, width, 128), BF16),
            pltpu.VMEM((32, 32, width), BF16),
            pltpu.VMEM((32, 32, width), BF16),
            pltpu.VMEM((2, UNITS, UNIT, 640), BF16),
            pltpu.VMEM((width, 128), BF16),
            pltpu.VMEM((2, LAT, 1152), BF16),
            pltpu.VMEM((2, LAT, VH), BF16),
            pltpu.VMEM((LAT, 1024), F32),
            pltpu.VMEM((8, 1024), F32),
            pltpu.VMEM((4, VH, 256), BF16),
            pltpu.VMEM((3, VH, 256), BF16),
            pltpu.VMEM((3, 8, 256), F32),
            pltpu.VMEM((3, 8, 256), F32),
            pltpu.VMEM((256, columns), BF16),
            pltpu.VMEM((columns, 256), BF16),
            pltpu.VMEM((256, 128), BF16),
            pltpu.VMEM((14, ZF, 128), BF16),
            pltpu.VMEM((14, ZF, 128), BF16),
            pltpu.VMEM((14, ZF, 128), BF16),
            pltpu.VMEM((14, ZF, 128), BF16),
            pltpu.VMEM((224, 128), F32),
            pltpu.VMEM((3, ZF, 128), BF16),
            pltpu.VMEM((3, ZF, 128), BF16),
            pltpu.VMEM((3, 8, YF, 128), BF16),
            pltpu.VMEM((3, 8, YF, 128), BF16),
            pltpu.VMEM((7, YF, 128), BF16),
            pltpu.VMEM((7, YF, 128), BF16),
            dma((6,)), dma((4,)), dma, dma((6,)), dma, dma((4, TURNS)), dma, dma((3,)), dma, dma((3,)),
            dma, dma((14,)), dma, dma((14,)), dma, dma((3,)), dma, dma((3, 5)), dma, dma((7,)),
        ],
        compiler_params=pltpu.CompilerParams(
            collective_id=0, has_side_effects=True, vmem_limit_bytes=56 * 2**20
        ),
        cost_estimate=pl.CostEstimate(flops=6 * 10**9, bytes_accessed=8 * 10**6, transcendentals=2 * 10**6),
    )(block_list[0, 0], cached_lengths, q, new, cache_pool[0], w_uv, w_o.reshape(256, columns))
    return mixed.T[None]


def solution(mesh):
    in_specs = (
        P("pool", "ctx", "head", None),
        P("pool", "ctx", None),
        P("ctx", "pool", None, None),
        P("pool", "ctx", None),
        P("pool"),
        P("head", None, None),
        P("head", None, None),
    )
    out_specs = P("pool", "ctx", "head")
    return jax.shard_map(body, mesh=mesh, in_specs=in_specs, out_specs=out_specs, check_vma=False)
```

```python
import jax
import jax.numpy as jnp
from jax import lax
from jax.experimental import pallas as pl
from jax.experimental.pallas import tpu as pltpu
from jax.sharding import PartitionSpec as P

MESH = pl.DeviceIdType.MESH
LAT = 512
VH = 128
UNIT = 32
UNITS = 1152 // UNIT
NEW_UNITS = 128 // UNIT
TURNS = UNITS // 4
HOP = 4
TILES = ((0, 384), (384, 896), (896, 1152))
SCALE = 192.0 ** -0.5 * 1.4426950408889634
NEG = -1e30
ZF, YF = 144, 80
Z_ORDER = (4, 3, 5, 2, 6, 1, 7, 0)
Z_GROUPS = ((0, 1), (1, 3), (3, 5), (5, 7), (7, 8))
F32 = jnp.float32
BF16 = jnp.bfloat16


def place():
    c, h, p = lax.axis_index("ctx"), lax.axis_index("head"), lax.axis_index("pool")
    return c // 2, c % 2, h // 4, h % 4, p


def device(x, yh, z, yl, p):
    return {"ctx": x * 2 + yh, "head": z * 4 + yl, "pool": p}


def greet(others):
    barrier = pltpu.get_barrier_semaphore()
    for other in others:
        pl.semaphore_signal(barrier, inc=1, device_id=other, device_id_type=MESH)
    pl.semaphore_wait(barrier, len(others))


def remote(src, dst, send, recv, to):
    return pltpu.make_async_remote_copy(
        src_ref=src, dst_ref=dst, send_sem=send, recv_sem=recv, device_id=to, device_id_type=MESH
    )


def kernel(
    blocks, cached_ref, q_in, new_in, pool_in, w_uv, w_in,
    out,
    qbuf, pbuf0, pbuf1, kbuf, newt, vt, wt, acc, stat, ores, orecv, sstat, srecv,
    w, wo, at, up_out, up_in, dn_out, dn_in, own, y_out, y_in, yf_out, yf_in, zf_out, zf_in,
    lsem, psem, qs, qr, ks, kr, os_, or_, ss, sr,
    us, ur, ds, dr, ys, yr, yfs, yfr, zfs, zfr,
):
    x, yh, z, yl, p = place()
    b = z % 2
    xu, xd, xo = (x + 1) % 4, (x + 3) % 4, (x + 2) % 4
    at_core = device(x, yh, z, yl, 1 - p)
    at_xu, at_xd, at_xo = [device(k, yh, z, yl, p) for k in (xu, xd, xo)]
    y_up, y_dn = (yh * 4 + yl + 1) % 8, (yh * 4 + yl + 7) % 8
    at_yu, at_yd = [device(x, k // 4, z, k % 4, p) for k in (y_up, y_dn)]
    at_z = [device(x, yh, (z + k) % 8, yl, p) for k in range(1, 8)]
    at_zu, at_zd = at_z[0], at_z[6]
    at_y = [device(x, yh, z, (yl + d) % 4, p) for d in (1, 2, 3)]
    cached = cached_ref[0]
    width = q_in.shape[1]
    half = 16

    mine = pl.ds(p * half, half)
    local = [
        pltpu.make_async_copy(pool_in.at[:, pl.ds(0, 32)], pbuf0.at[mine], lsem.at[0]),
        pltpu.make_async_copy(pool_in.at[:, pl.ds(32, 32)], pbuf1.at[mine], lsem.at[5]),
        pltpu.make_async_copy(q_in, qbuf.at[0], lsem.at[1]),
        pltpu.make_async_copy(new_in, newt, lsem.at[2]),
    ]
    load_w = pltpu.make_async_copy(w_in, w, lsem.at[3])
    load_uv = pltpu.make_async_copy(w_uv, wt, lsem.at[4])
    for copy in local + [load_uv, load_w]:
        copy.start()
    greet([at_core, at_xu, at_xd, at_xo, at_yu, at_yd] + at_z + at_y)

    push = []
    for i, pbuf in enumerate((pbuf0, pbuf1)):
        rows = pl.ds(i * 32, 32)
        push.append(remote(pool_in.at[:, rows], pbuf.at[mine], psem.at[i], psem.at[2 + i], at_core))
        push[i].start()
    q_up = [remote(q_in.at[h], qbuf.at[1, h], qs, qr.at[h], at_xu) for h in range(2)]
    q_dn = [remote(q_in.at[h], qbuf.at[2, h], qs, qr.at[2 + h], at_xd) for h in range(2)]
    for copy in (q_up[0], q_dn[1], q_up[1], q_dn[0]):
        copy.start()
    q_up2 = remote(qbuf.at[1, 0], qbuf.at[3, 0], qs, qr.at[4], at_xu)
    q_dn2 = remote(qbuf.at[2, 1], qbuf.at[3, 1], qs, qr.at[5], at_xd)

    for copy in local:
        copy.wait()
    kbuf[0, :, :, width:] = jnp.zeros((UNITS, UNIT, kbuf.shape[-1] - width), BF16)
    kbuf[0, 0:NEW_UNITS, :, :width] = newt[...].T.reshape(NEW_UNITS, UNIT, width)

    def y_up_copy(s, j):
        u = j * 4 + b * 2
        return remote(kbuf.at[s, u], kbuf.at[1, u], ks, kr.at[0, j], at_yu)

    def y_dn_copy(s, j):
        u = j * 4 + b * 2 + 1
        return remote(kbuf.at[s, u], kbuf.at[1, u], ks, kr.at[1, j], at_yd)

    def z_up_copy(j, base):
        u = j * 4 + base * 2
        return remote(kbuf.at[1, u], kbuf.at[1, u], ks, kr.at[2, j], at_zu)

    def z_dn_copy(j, base):
        u = j * 4 + base * 2 + 1
        return remote(kbuf.at[1, u], kbuf.at[1, u], ks, kr.at[3, j], at_zd)

    def first(lo, hi):
        @pl.when(yl == 3)
        def _():
            for j in range(lo, hi):
                y_up_copy(0, j).start()

        @pl.when(yl == 0)
        def _():
            for j in range(lo, hi):
                y_dn_copy(0, j).start()

    first(0, NEW_UNITS // 4)
    per_half = half * 32 // UNIT
    for i, pbuf in enumerate((pbuf0, pbuf1)):
        push[i].wait_recv()

        def gather(k, carry):
            u = NEW_UNITS + i * per_half + k * (32 // UNIT)
            kbuf[0, pl.ds(u, 32 // UNIT), :, :width] = pbuf[blocks[k]].reshape(32 // UNIT, UNIT, width)
            return carry

        lax.fori_loop(0, half, gather, 0)
        first((NEW_UNITS + i * per_half) // 4, (NEW_UNITS + (i + 1) * per_half) // 4)

    def forward(step):
        j = step - HOP * (yl + 1)

        @pl.when((j >= 0) & (j < TURNS))
        def _():
            y_up_copy(1, j).wait_recv()

            @pl.when(yl != 3)
            def _():
                y_up_copy(1, j).start()

            z_up_copy(j, b).start()

        k = step - HOP * (4 - yl)

        @pl.when((k >= 0) & (k < TURNS))
        def _():
            y_dn_copy(1, k).wait_recv()

            @pl.when(yl != 0)
            def _():
                y_dn_copy(1, k).start()

            z_dn_copy(k, b).start()

    owners = [x, xd, xu, xo]

    def attend(slots, s_at, tile):
        c = x * 2 + (yh if s_at == 0 else 1 - yh)
        lo, lanes = slots[0] * 256, len(slots) * 256
        cols = slice(lo, lo + lanes)
        begin, end = TILES[tile]
        rows = end - begin
        keys = kbuf[s_at, begin // UNIT:end // UNIT].reshape(rows, kbuf.shape[-1])[:, :width]
        query = jnp.concatenate([qbuf[g, h] for g in slots for h in range(2)], axis=1)
        s = jnp.dot(keys, query, preferred_element_type=F32) * SCALE
        new = 0 if tile else 128
        row = lax.broadcasted_iota(jnp.int32, (rows - new, lanes), 0) + (begin + new - 128)
        row = ((row >> 5) & 15) * 64 + (row >> 9) * 32 + (row & 31)
        s_hist = jnp.where(row < cached - c * 1024, s[new:], NEG)
        if new:
            token = lax.broadcasted_iota(jnp.int32, (1, 256), 1) % 128
            last = jnp.concatenate([token + (owners[g] * 2 + yh - c) * 128 for g in slots], axis=1)
            row = lax.broadcasted_iota(jnp.int32, (128, lanes), 0)
            s = jnp.concatenate([jnp.where(row <= last, s[:new], NEG), s_hist], axis=0)
        else:
            s = s_hist
        fresh = s_at == 0 and tile == 0
        top = jnp.max(s, axis=0, keepdims=True)
        if not fresh:
            old = stat[0:1, cols]
            top = jnp.maximum(top, old)
        e = jnp.exp2(s - top)
        total = jnp.sum(e, axis=0, keepdims=True)
        o = jnp.dot(vt[s_at, :, begin:end], e.astype(BF16), preferred_element_type=F32)
        if not fresh:
            f = jnp.exp2(old - top)
            total = total + f * stat[1:2, cols]
            o = o + f * acc[:, cols]
        stat[0:1, cols] = top
        stat[1:2, cols] = total
        acc[:, cols] = o

    def turn(s_at, tile):
        begin, end = TILES[tile]
        v = kbuf[s_at, begin // UNIT:end // UNIT].reshape(end - begin, kbuf.shape[-1])[:, :LAT]
        vt[s_at, :, begin:end] = v.T

    def turn_w(i):
        wo[i * 896:(i + 1) * 896] = w[:, i * 896:(i + 1) * 896].T

    near, far = (0, 1), (2, 3)
    for t in range(3):
        turn(0, t)
    q_up[0].wait_recv()
    q_up2.start()
    q_dn[1].wait_recv()
    q_dn2.start()
    load_w.wait()
    load_uv.wait()
    for step in range(HOP, 4 * HOP + TURNS):
        forward(step)
        if step == round(6 * HOP / 4):
            q_up[1].wait_recv()
        if step == round(10 * HOP / 4):
            q_dn[0].wait_recv()
            q_up2.wait_recv()
            q_dn2.wait_recv()
        for t in range(3):
            if step == round((6 + t) * HOP / 4):
                attend(near, 0, t)
            if step == round((10 + t) * HOP / 4):
                attend(far, 0, t)
        for t in range(8):
            if step == round((4 + t if t < 2 else 11 + t) * HOP / 4):
                turn_w(t)

    def landed(tile):
        begin, end = TILES[tile]
        for j in range(begin // UNIT // 4, end // UNIT // 4):
            z_up_copy(j, 1 - b).wait_recv()
            z_dn_copy(j, 1 - b).wait_recv()
        turn(1, tile)

    for tile in range(3):
        landed(tile)
        attend(near + far, 1, tile)

    results = []
    for g in (3, 1, 2, 0):
        cols = slice(g * 256, (g + 1) * 256)
        lat = (acc[:, cols] * (1.0 / stat[1:2, cols])).astype(BF16)
        for h in range(2):
            o = lax.dot_general(
                wt[h], lat[:, h * 128:(h + 1) * 128], (((0,), (0,)), ((), ())), preferred_element_type=F32
            )
            ores[g, :, h * 128:(h + 1) * 128] = o.astype(BF16)
        if g:
            sstat[g - 1, 0:2] = stat[0:2, cols]
            to = {1: at_xd, 2: at_xu, 3: at_xo}[g]
            sent = [
                remote(ores.at[g], orecv.at[g - 1], os_, or_.at[g - 1], to),
                remote(sstat.at[g - 1], srecv.at[g - 1], ss, sr.at[g - 1], to),
            ]
            for copy in sent:
                copy.start()
            results += sent

    for copy in results:
        copy.wait_recv()
    tops = [stat[0:1, 0:256]] + [srecv[i, 0:1] for i in range(3)]
    sums = [stat[1:2, 0:256]] + [srecv[i, 1:2] for i in range(3)]
    outs = [ores[0]] + [orecv[i] for i in range(3)]
    top = jnp.maximum(jnp.maximum(tops[0], tops[1]), jnp.maximum(tops[2], tops[3]))
    shares = [t * jnp.exp2(m - top) for m, t in zip(tops, sums)]
    inv = 1.0 / (shares[0] + shares[1] + shares[2] + shares[3])
    head = sum(o.astype(F32) * (s * inv) for o, s in zip(outs, shares))
    for h in range(2):
        at[h * 128:(h + 1) * 128] = head[:, h * 128:(h + 1) * 128].astype(BF16)

    a = at[...]

    def term(dest, d, lo, rows):
        row = pl.multiple_of((dest % 8) * 896 + ((yl + 1 + d) % 4) * 224 + lo, 16)
        return jnp.dot(wo[pl.ds(row, rows)], a, preferred_element_type=F32)

    def slot(s, d):
        return s * 4 - 2 + d if s else d % 2

    def flow(way, s, d):
        i = slot(s, d)
        if way == "up":
            return remote(up_out.at[i], up_in.at[i], us, ur.at[i], at_zu)
        return remote(dn_out.at[i], dn_in.at[i], ds, dr.at[i], at_zd)

    def ring(s, order):
        own_terms = [term(z + 4 - s if way == "up" else z + 4 + s, d, 0, ZF) for way, d in order]
        for (way, d), v in zip(order, own_terms):
            sent, got = (up_out, up_in) if way == "up" else (dn_out, dn_in)
            if s > 1 or (s == 1 and (d >= 2) == (way == "up")):
                flow(way, s - 1, d).wait_recv()
                v = v + got[slot(s - 1, d)].astype(F32)
            sent[slot(s, d)] = v.astype(BF16)
            flow(way, s, d).start()

    def y_first(g, d):
        lo, hi = Z_GROUPS[g]
        rows = pl.ds(lo, hi - lo)
        return remote(yf_out.at[d, rows], yf_in.at[d, rows], yfs, yfr.at[d, g], at_y[d])

    def send_group(g):
        for d in range(3):
            for i in range(*Z_GROUPS[g]):
                yf_out[d, i] = term(z + Z_ORDER[i], d, ZF, YF).astype(BF16)
            y_first(g, d).start()

    def z_last(i):
        to = device(x, yh, (z + Z_ORDER[i]) % 8, yl, p)
        return remote(zf_out.at[i], zf_in.at[i], zfs, zfr.at[i], to)

    def take_group(g):
        members = range(*Z_GROUPS[g])
        own_terms = [term(z + Z_ORDER[i], 3, ZF, YF) for i in members]
        for d in range(3):
            y_first(g, d).wait_recv()
        for i, v in zip(members, own_terms):
            for d in range(3):
                v = v + yf_in[d, i].astype(F32)
            if Z_ORDER[i]:
                zf_out[i] = v.astype(BF16)
                z_last(i).start()
            else:
                own[ZF:] = v

    def y_last(d):
        return remote(y_out.at[d], y_in.at[d], ys, yr.at[d], at_y[d])

    ring(0, (("up", 2), ("dn", 0), ("up", 3), ("dn", 1)))
    send_group(0)
    ring(1, (("up", 0), ("dn", 2), ("up", 1), ("dn", 3)))
    send_group(1)
    ring(1, (("dn", 0), ("up", 2), ("dn", 1), ("up", 3)))
    send_group(2)
    send_group(3)
    ring(2, (("up", 0), ("dn", 2), ("up", 1), ("dn", 3)))
    take_group(0)
    send_group(4)
    ring(2, (("up", 2), ("dn", 0), ("up", 3), ("dn", 1)))
    take_group(1)
    ring(3, (("up", 0), ("dn", 2), ("up", 1), ("dn", 0)))
    take_group(2)
    ring(3, (("up", 2), ("dn", 1), ("up", 3), ("dn", 3)))
    take_group(3)
    order = (0, 2, 1, 3)
    own_terms = [term(z, d, 0, ZF) for d in order]
    for d, v in zip(order, own_terms):
        flow("up", 3, d).wait_recv()
        flow("dn", 3, d).wait_recv()
        i = slot(3, d)
        v = v + up_in[i].astype(F32) + dn_in[i].astype(F32)
        if d < 3:
            y_out[d] = v.astype(BF16)
            y_last(d).start()
        else:
            own[:ZF] = v
    take_group(4)
    v = own[ZF:]
    for i in range(7):
        z_last(i).wait_recv()
        v = v + zf_in[i].astype(F32)
    out[ZF:] = v.astype(BF16)
    v = own[:ZF]
    for d in range(3):
        y_last(d).wait_recv()
        v = v + y_in[d].astype(F32)
    out[:ZF] = v.astype(BF16)

    for copy in push:
        copy.wait_send()
    for ref, sem in (
        (qbuf.at[pl.ds(0, 3)], qs), (kbuf.at[1], ks), (orecv, os_), (srecv, ss), (up_out, us), (dn_out, ds),
        (yf_out, yfs), (zf_out, zfs), (y_out, ys),
    ):
        pltpu.make_async_copy(ref, ref, sem).wait()


def body(queries, new_latent, cache_pool, block_list, cached_lengths, w_uv, w_o):
    width = queries.shape[-1]
    columns = w_o.shape[-1]
    q = jnp.transpose(queries[0], (1, 2, 0))
    new = new_latent[0].T
    hbm = pl.BlockSpec(memory_space=pltpu.HBM)
    smem = pl.BlockSpec(memory_space=pltpu.SMEM)
    dma = pltpu.SemaphoreType.DMA
    mixed = pl.pallas_call(
        kernel,
        out_shape=jax.ShapeDtypeStruct((224, 128), BF16),
        in_specs=[smem, smem, hbm, hbm, hbm, hbm, hbm],
        out_specs=pl.BlockSpec(memory_space=pltpu.VMEM),
        scratch_shapes=[
            pltpu.VMEM((4, 2, width, 128), BF16),
            pltpu.VMEM((32, 32, width), BF16),
            pltpu.VMEM((32, 32, width), BF16),
            pltpu.VMEM((2, UNITS, UNIT, 640), BF16),
            pltpu.VMEM((width, 128), BF16),
            pltpu.VMEM((2, LAT, 1152), BF16),
            pltpu.VMEM((2, LAT, VH), BF16),
            pltpu.VMEM((LAT, 1024), F32),
            pltpu.VMEM((8, 1024), F32),
            pltpu.VMEM((4, VH, 256), BF16),
            pltpu.VMEM((3, VH, 256), BF16),
            pltpu.VMEM((3, 8, 256), F32),
            pltpu.VMEM((3, 8, 256), F32),
            pltpu.VMEM((256, columns), BF16),
            pltpu.VMEM((columns, 256), BF16),
            pltpu.VMEM((256, 128), BF16),
            pltpu.VMEM((14, ZF, 128), BF16),
            pltpu.VMEM((14, ZF, 128), BF16),
            pltpu.VMEM((14, ZF, 128), BF16),
            pltpu.VMEM((14, ZF, 128), BF16),
            pltpu.VMEM((224, 128), F32),
            pltpu.VMEM((3, ZF, 128), BF16),
            pltpu.VMEM((3, ZF, 128), BF16),
            pltpu.VMEM((3, 8, YF, 128), BF16),
            pltpu.VMEM((3, 8, YF, 128), BF16),
            pltpu.VMEM((7, YF, 128), BF16),
            pltpu.VMEM((7, YF, 128), BF16),
            dma((6,)), dma((4,)), dma, dma((6,)), dma, dma((4, TURNS)), dma, dma((3,)), dma, dma((3,)),
            dma, dma((14,)), dma, dma((14,)), dma, dma((3,)), dma, dma((3, 5)), dma, dma((7,)),
        ],
        compiler_params=pltpu.CompilerParams(
            collective_id=0, has_side_effects=True, vmem_limit_bytes=56 * 2**20
        ),
        cost_estimate=pl.CostEstimate(flops=6 * 10**9, bytes_accessed=8 * 10**6, transcendentals=2 * 10**6),
    )(block_list[0, 0], cached_lengths, q, new, cache_pool[0], w_uv, w_o.reshape(256, columns))
    return mixed.T[None]


def solution(mesh):
    in_specs = (
        P("pool", "ctx", "head", None),
        P("pool", "ctx", None),
        P("ctx", "pool", None, None),
        P("pool", "ctx", None),
        P("pool"),
        P("head", None, None),
        P("head", None, None),
    )
    out_specs = P("pool", "ctx", "head")
    return jax.shard_map(body, mesh=mesh, in_specs=in_specs, out_specs=out_specs, check_vma=False)
```

```python
import jax
import jax.numpy as jnp
from jax import lax
from jax.experimental import pallas as pl
from jax.experimental.pallas import tpu as pltpu
from jax.sharding import PartitionSpec as P

MESH = pl.DeviceIdType.MESH
LAT = 512
VH = 128
UNIT = 32
UNITS = 1152 // UNIT
NEW_UNITS = 128 // UNIT
TURNS = UNITS // 4
HOP = 4
TILES = ((0, 384), (384, 896), (896, 1152))
SCALE = 192.0 ** -0.5 * 1.4426950408889634
NEG = -1e30
ZF, YF = 144, 80
Z_ORDER = (4, 3, 5, 2, 6, 1, 7, 0)
Z_GROUPS = ((0, 1), (1, 3), (3, 5), (5, 7), (7, 8))
F32 = jnp.float32
BF16 = jnp.bfloat16


def place():
    c, h, p = lax.axis_index("ctx"), lax.axis_index("head"), lax.axis_index("pool")
    return c // 2, c % 2, h // 4, h % 4, p


def device(x, yh, z, yl, p):
    return {"ctx": x * 2 + yh, "head": z * 4 + yl, "pool": p}


def greet(others):
    barrier = pltpu.get_barrier_semaphore()
    for other in others:
        pl.semaphore_signal(barrier, inc=1, device_id=other, device_id_type=MESH)
    pl.semaphore_wait(barrier, len(others))


def remote(src, dst, send, recv, to):
    return pltpu.make_async_remote_copy(
        src_ref=src, dst_ref=dst, send_sem=send, recv_sem=recv, device_id=to, device_id_type=MESH
    )


def kernel(
    blocks, cached_ref, q_in, new_in, pool_in, w_uv, w_in,
    out,
    qbuf, pbuf0, pbuf1, kbuf, newt, vt, wt, acc, stat, ores, orecv, sstat, srecv,
    w, wo, at, up_out, up_in, dn_out, dn_in, own, y_out, y_in, yf_out, yf_in, zf_out, zf_in,
    lsem, psem, qs, qr, ks, kr, os_, or_, ss, sr,
    us, ur, ds, dr, ys, yr, yfs, yfr, zfs, zfr,
):
    x, yh, z, yl, p = place()
    b = z % 2
    xu, xd, xo = (x + 1) % 4, (x + 3) % 4, (x + 2) % 4
    at_core = device(x, yh, z, yl, 1 - p)
    at_xu, at_xd, at_xo = [device(k, yh, z, yl, p) for k in (xu, xd, xo)]
    y_up, y_dn = (yh * 4 + yl + 1) % 8, (yh * 4 + yl + 7) % 8
    at_yu, at_yd = [device(x, k // 4, z, k % 4, p) for k in (y_up, y_dn)]
    at_z = [device(x, yh, (z + k) % 8, yl, p) for k in range(1, 8)]
    at_zu, at_zd = at_z[0], at_z[6]
    at_y = [device(x, yh, z, (yl + d) % 4, p) for d in (1, 2, 3)]
    cached = cached_ref[0]
    width = q_in.shape[1]
    half = 16

    mine = pl.ds(p * half, half)
    local = [
        pltpu.make_async_copy(pool_in.at[:, pl.ds(0, 32)], pbuf0.at[mine], lsem.at[0]),
        pltpu.make_async_copy(pool_in.at[:, pl.ds(32, 32)], pbuf1.at[mine], lsem.at[5]),
        pltpu.make_async_copy(q_in, qbuf.at[0], lsem.at[1]),
        pltpu.make_async_copy(new_in, newt, lsem.at[2]),
    ]
    load_w = pltpu.make_async_copy(w_in, w, lsem.at[3])
    load_uv = pltpu.make_async_copy(w_uv, wt, lsem.at[4])
    for copy in local + [load_uv, load_w]:
        copy.start()
    greet([at_core, at_xu, at_xd, at_xo, at_yu, at_yd] + at_z + at_y)

    push = []
    for i, pbuf in enumerate((pbuf0, pbuf1)):
        rows = pl.ds(i * 32, 32)
        push.append(remote(pool_in.at[:, rows], pbuf.at[mine], psem.at[i], psem.at[2 + i], at_core))
        push[i].start()
    q_up = [remote(q_in.at[h], qbuf.at[1, h], qs, qr.at[h], at_xu) for h in range(2)]
    q_dn = [remote(q_in.at[h], qbuf.at[2, h], qs, qr.at[2 + h], at_xd) for h in range(2)]
    for copy in (q_up[0], q_dn[1], q_up[1], q_dn[0]):
        copy.start()
    q_up2 = remote(qbuf.at[1, 0], qbuf.at[3, 0], qs, qr.at[4], at_xu)
    q_dn2 = remote(qbuf.at[2, 1], qbuf.at[3, 1], qs, qr.at[5], at_xd)

    for copy in local:
        copy.wait()
    kbuf[0, :, :, width:] = jnp.zeros((UNITS, UNIT, kbuf.shape[-1] - width), BF16)
    kbuf[0, 0:NEW_UNITS, :, :width] = newt[...].T.reshape(NEW_UNITS, UNIT, width)

    def y_up_copy(s, j):
        u = j * 4 + b * 2
        return remote(kbuf.at[s, u], kbuf.at[1, u], ks, kr.at[0, j], at_yu)

    def y_dn_copy(s, j):
        u = j * 4 + b * 2 + 1
        return remote(kbuf.at[s, u], kbuf.at[1, u], ks, kr.at[1, j], at_yd)

    def z_up_copy(j, base):
        u = j * 4 + base * 2
        return remote(kbuf.at[1, u], kbuf.at[1, u], ks, kr.at[2, j], at_zu)

    def z_dn_copy(j, base):
        u = j * 4 + base * 2 + 1
        return remote(kbuf.at[1, u], kbuf.at[1, u], ks, kr.at[3, j], at_zd)

    def first(lo, hi):
        @pl.when(yl == 3)
        def _():
            for j in range(lo, hi):
                y_up_copy(0, j).start()

        @pl.when(yl == 0)
        def _():
            for j in range(lo, hi):
                y_dn_copy(0, j).start()

    first(0, NEW_UNITS // 4)
    per_half = half * 32 // UNIT
    for i, pbuf in enumerate((pbuf0, pbuf1)):
        push[i].wait_recv()

        def gather(k, carry):
            u = NEW_UNITS + i * per_half + k * (32 // UNIT)
            kbuf[0, pl.ds(u, 32 // UNIT), :, :width] = pbuf[blocks[k]].reshape(32 // UNIT, UNIT, width)
            return carry

        lax.fori_loop(0, half, gather, 0)
        first((NEW_UNITS + i * per_half) // 4, (NEW_UNITS + (i + 1) * per_half) // 4)

    def forward(step):
        j = step - HOP * (yl + 1)

        @pl.when((j >= 0) & (j < TURNS))
        def _():
            y_up_copy(1, j).wait_recv()

            @pl.when(yl != 3)
            def _():
                y_up_copy(1, j).start()

            z_up_copy(j, b).start()

        k = step - HOP * (4 - yl)

        @pl.when((k >= 0) & (k < TURNS))
        def _():
            y_dn_copy(1, k).wait_recv()

            @pl.when(yl != 0)
            def _():
                y_dn_copy(1, k).start()

            z_dn_copy(k, b).start()

    owners = [x, xd, xu, xo]

    def attend(slots, s_at, tile):
        c = x * 2 + (yh if s_at == 0 else 1 - yh)
        lo, lanes = slots[0] * 256, len(slots) * 256
        cols = slice(lo, lo + lanes)
        begin, end = TILES[tile]
        rows = end - begin
        keys = kbuf[s_at, begin // UNIT:end // UNIT].reshape(rows, kbuf.shape[-1])[:, :width]
        query = jnp.concatenate([qbuf[g, h] for g in slots for h in range(2)], axis=1)
        s = jnp.dot(keys, query, preferred_element_type=F32) * SCALE
        new = 0 if tile else 128
        row = lax.broadcasted_iota(jnp.int32, (rows - new, lanes), 0) + (begin + new - 128)
        row = ((row >> 5) & 15) * 64 + (row >> 9) * 32 + (row & 31)
        s_hist = jnp.where(row < cached - c * 1024, s[new:], NEG)
        if new:
            token = lax.broadcasted_iota(jnp.int32, (1, 256), 1) % 128
            last = jnp.concatenate([token + (owners[g] * 2 + yh - c) * 128 for g in slots], axis=1)
            row = lax.broadcasted_iota(jnp.int32, (128, lanes), 0)
            s = jnp.concatenate([jnp.where(row <= last, s[:new], NEG), s_hist], axis=0)
        else:
            s = s_hist
        fresh = s_at == 0 and tile == 0
        top = jnp.max(s, axis=0, keepdims=True)
        if not fresh:
            old = stat[0:1, cols]
            top = jnp.maximum(top, old)
        e = jnp.exp2(s - top)
        total = jnp.sum(e, axis=0, keepdims=True)
        o = jnp.dot(vt[s_at, :, begin:end], e.astype(BF16), preferred_element_type=F32)
        if not fresh:
            f = jnp.exp2(old - top)
            total = total + f * stat[1:2, cols]
            o = o + f * acc[:, cols]
        stat[0:1, cols] = top
        stat[1:2, cols] = total
        acc[:, cols] = o

    def turn(s_at, tile):
        begin, end = TILES[tile]
        v = kbuf[s_at, begin // UNIT:end // UNIT].reshape(end - begin, kbuf.shape[-1])[:, :LAT]
        vt[s_at, :, begin:end] = v.T

    def turn_w(i):
        wo[i * 896:(i + 1) * 896] = w[:, i * 896:(i + 1) * 896].T

    near, far = (0, 1), (2, 3)
    for t in range(3):
        turn(0, t)
    q_up[0].wait_recv()
    q_up2.start()
    q_dn[1].wait_recv()
    q_dn2.start()
    load_w.wait()
    load_uv.wait()
    for step in range(HOP, 4 * HOP + TURNS):
        forward(step)
        if step == round(6 * HOP / 4):
            q_up[1].wait_recv()
        if step == round(10 * HOP / 4):
            q_dn[0].wait_recv()
            q_up2.wait_recv()
            q_dn2.wait_recv()
        for t in range(3):
            if step == round((6 + t) * HOP / 4):
                attend(near, 0, t)
            if step == round((10 + t) * HOP / 4):
                attend(far, 0, t)
        for t in range(8):
            if step == round((4 + t // 2) * HOP / 4):
                turn_w(t)

    def landed(tile):
        begin, end = TILES[tile]
        for j in range(begin // UNIT // 4, end // UNIT // 4):
            z_up_copy(j, 1 - b).wait_recv()
            z_dn_copy(j, 1 - b).wait_recv()
        turn(1, tile)

    for tile in range(3):
        landed(tile)
        attend(near + far, 1, tile)

    results = []
    for g in (3, 1, 2, 0):
        cols = slice(g * 256, (g + 1) * 256)
        lat = (acc[:, cols] * (1.0 / stat[1:2, cols])).astype(BF16)
        for h in range(2):
            o = lax.dot_general(
                wt[h], lat[:, h * 128:(h + 1) * 128], (((0,), (0,)), ((), ())), preferred_element_type=F32
            )
            ores[g, :, h * 128:(h + 1) * 128] = o.astype(BF16)
        if g:
            sstat[g - 1, 0:2] = stat[0:2, cols]
            to = {1: at_xd, 2: at_xu, 3: at_xo}[g]
            sent = [
                remote(ores.at[g], orecv.at[g - 1], os_, or_.at[g - 1], to),
                remote(sstat.at[g - 1], srecv.at[g - 1], ss, sr.at[g - 1], to),
            ]
            for copy in sent:
                copy.start()
            results += sent

    for copy in results:
        copy.wait_recv()
    tops = [stat[0:1, 0:256]] + [srecv[i, 0:1] for i in range(3)]
    sums = [stat[1:2, 0:256]] + [srecv[i, 1:2] for i in range(3)]
    outs = [ores[0]] + [orecv[i] for i in range(3)]
    top = jnp.maximum(jnp.maximum(tops[0], tops[1]), jnp.maximum(tops[2], tops[3]))
    shares = [t * jnp.exp2(m - top) for m, t in zip(tops, sums)]
    inv = 1.0 / (shares[0] + shares[1] + shares[2] + shares[3])
    head = sum(o.astype(F32) * (s * inv) for o, s in zip(outs, shares))
    for h in range(2):
        at[h * 128:(h + 1) * 128] = head[:, h * 128:(h + 1) * 128].astype(BF16)

    a = at[...]

    def term(dest, d, lo, rows):
        row = pl.multiple_of((dest % 8) * 896 + ((yl + 1 + d) % 4) * 224 + lo, 16)
        return jnp.dot(wo[pl.ds(row, rows)], a, preferred_element_type=F32)

    def slot(s, d):
        return s * 4 - 2 + d if s else d % 2

    def flow(way, s, d):
        i = slot(s, d)
        if way == "up":
            return remote(up_out.at[i], up_in.at[i], us, ur.at[i], at_zu)
        return remote(dn_out.at[i], dn_in.at[i], ds, dr.at[i], at_zd)

    def ring(s, order):
        own_terms = [term(z + 4 - s if way == "up" else z + 4 + s, d, 0, ZF) for way, d in order]
        for (way, d), v in zip(order, own_terms):
            sent, got = (up_out, up_in) if way == "up" else (dn_out, dn_in)
            if s > 1 or (s == 1 and (d >= 2) == (way == "up")):
                flow(way, s - 1, d).wait_recv()
                v = v + got[slot(s - 1, d)].astype(F32)
            sent[slot(s, d)] = v.astype(BF16)
            flow(way, s, d).start()

    def y_first(g, d):
        lo, hi = Z_GROUPS[g]
        rows = pl.ds(lo, hi - lo)
        return remote(yf_out.at[d, rows], yf_in.at[d, rows], yfs, yfr.at[d, g], at_y[d])

    def send_group(g):
        for d in range(3):
            for i in range(*Z_GROUPS[g]):
                yf_out[d, i] = term(z + Z_ORDER[i], d, ZF, YF).astype(BF16)
            y_first(g, d).start()

    def z_last(i):
        to = device(x, yh, (z + Z_ORDER[i]) % 8, yl, p)
        return remote(zf_out.at[i], zf_in.at[i], zfs, zfr.at[i], to)

    def take_group(g):
        members = range(*Z_GROUPS[g])
        own_terms = [term(z + Z_ORDER[i], 3, ZF, YF) for i in members]
        for d in range(3):
            y_first(g, d).wait_recv()
        for i, v in zip(members, own_terms):
            for d in range(3):
                v = v + yf_in[d, i].astype(F32)
            if Z_ORDER[i]:
                zf_out[i] = v.astype(BF16)
                z_last(i).start()
            else:
                own[ZF:] = v

    def y_last(d):
        return remote(y_out.at[d], y_in.at[d], ys, yr.at[d], at_y[d])

    ring(0, (("up", 2), ("dn", 0), ("up", 3), ("dn", 1)))
    send_group(0)
    ring(1, (("up", 0), ("dn", 2), ("up", 1), ("dn", 3)))
    send_group(1)
    ring(1, (("dn", 0), ("up", 2), ("dn", 1), ("up", 3)))
    send_group(2)
    send_group(3)
    ring(2, (("up", 0), ("dn", 2), ("up", 1), ("dn", 3)))
    take_group(0)
    send_group(4)
    ring(2, (("up", 2), ("dn", 0), ("up", 3), ("dn", 1)))
    take_group(1)
    ring(3, (("up", 0), ("dn", 2), ("up", 1), ("dn", 0)))
    take_group(2)
    ring(3, (("up", 2), ("dn", 1), ("up", 3), ("dn", 3)))
    take_group(3)
    order = (0, 2, 1, 3)
    own_terms = [term(z, d, 0, ZF) for d in order]
    for d, v in zip(order, own_terms):
        flow("up", 3, d).wait_recv()
        flow("dn", 3, d).wait_recv()
        i = slot(3, d)
        v = v + up_in[i].astype(F32) + dn_in[i].astype(F32)
        if d < 3:
            y_out[d] = v.astype(BF16)
            y_last(d).start()
        else:
            own[:ZF] = v
    take_group(4)
    v = own[ZF:]
    for i in range(7):
        z_last(i).wait_recv()
        v = v + zf_in[i].astype(F32)
    out[ZF:] = v.astype(BF16)
    v = own[:ZF]
    for d in range(3):
        y_last(d).wait_recv()
        v = v + y_in[d].astype(F32)
    out[:ZF] = v.astype(BF16)

    for copy in push:
        copy.wait_send()
    for ref, sem in (
        (qbuf.at[pl.ds(0, 3)], qs), (kbuf.at[1], ks), (orecv, os_), (srecv, ss), (up_out, us), (dn_out, ds),
        (yf_out, yfs), (zf_out, zfs), (y_out, ys),
    ):
        pltpu.make_async_copy(ref, ref, sem).wait()


def body(queries, new_latent, cache_pool, block_list, cached_lengths, w_uv, w_o):
    width = queries.shape[-1]
    columns = w_o.shape[-1]
    q = jnp.transpose(queries[0], (1, 2, 0))
    new = new_latent[0].T
    hbm = pl.BlockSpec(memory_space=pltpu.HBM)
    smem = pl.BlockSpec(memory_space=pltpu.SMEM)
    dma = pltpu.SemaphoreType.DMA
    mixed = pl.pallas_call(
        kernel,
        out_shape=jax.ShapeDtypeStruct((224, 128), BF16),
        in_specs=[smem, smem, hbm, hbm, hbm, hbm, hbm],
        out_specs=pl.BlockSpec(memory_space=pltpu.VMEM),
        scratch_shapes=[
            pltpu.VMEM((4, 2, width, 128), BF16),
            pltpu.VMEM((32, 32, width), BF16),
            pltpu.VMEM((32, 32, width), BF16),
            pltpu.VMEM((2, UNITS, UNIT, 640), BF16),
            pltpu.VMEM((width, 128), BF16),
            pltpu.VMEM((2, LAT, 1152), BF16),
            pltpu.VMEM((2, LAT, VH), BF16),
            pltpu.VMEM((LAT, 1024), F32),
            pltpu.VMEM((8, 1024), F32),
            pltpu.VMEM((4, VH, 256), BF16),
            pltpu.VMEM((3, VH, 256), BF16),
            pltpu.VMEM((3, 8, 256), F32),
            pltpu.VMEM((3, 8, 256), F32),
            pltpu.VMEM((256, columns), BF16),
            pltpu.VMEM((columns, 256), BF16),
            pltpu.VMEM((256, 128), BF16),
            pltpu.VMEM((14, ZF, 128), BF16),
            pltpu.VMEM((14, ZF, 128), BF16),
            pltpu.VMEM((14, ZF, 128), BF16),
            pltpu.VMEM((14, ZF, 128), BF16),
            pltpu.VMEM((224, 128), F32),
            pltpu.VMEM((3, ZF, 128), BF16),
            pltpu.VMEM((3, ZF, 128), BF16),
            pltpu.VMEM((3, 8, YF, 128), BF16),
            pltpu.VMEM((3, 8, YF, 128), BF16),
            pltpu.VMEM((7, YF, 128), BF16),
            pltpu.VMEM((7, YF, 128), BF16),
            dma((6,)), dma((4,)), dma, dma((6,)), dma, dma((4, TURNS)), dma, dma((3,)), dma, dma((3,)),
            dma, dma((14,)), dma, dma((14,)), dma, dma((3,)), dma, dma((3, 5)), dma, dma((7,)),
        ],
        compiler_params=pltpu.CompilerParams(
            collective_id=0, has_side_effects=True, vmem_limit_bytes=56 * 2**20
        ),
        cost_estimate=pl.CostEstimate(flops=6 * 10**9, bytes_accessed=8 * 10**6, transcendentals=2 * 10**6),
    )(block_list[0, 0], cached_lengths, q, new, cache_pool[0], w_uv, w_o.reshape(256, columns))
    return mixed.T[None]


def solution(mesh):
    in_specs = (
        P("pool", "ctx", "head", None),
        P("pool", "ctx", None),
        P("ctx", "pool", None, None),
        P("pool", "ctx", None),
        P("pool"),
        P("head", None, None),
        P("head", None, None),
    )
    out_specs = P("pool", "ctx", "head")
    return jax.shard_map(body, mesh=mesh, in_specs=in_specs, out_specs=out_specs, check_vma=False)
```
